32 devices in a mesh: ctx: 8 (over y, x, core), tp: 4 (over z).
Axes of the slice: x: 2, y: 2, z: 4, core: 2. Of those that a mesh axis runs over, the one named last changes fastest.
Arguments:
- queries: bfloat16 [2048, 2048], P('ctx', 'tp'), may hold values from -6 to 6
- keys_copied: bfloat16 [2048, 512], P('ctx', 'tp'), may hold values from -6 to 6, as said below
- values_copied: bfloat16 [2048, 512], P('ctx', 'tp'), may hold values from -6 to 6, as said below
- attention_output_saved: bfloat16 [2048, 2048], P('ctx', 'tp'), may hold values from -6 to 6
- log_norm: float32 [16, 2048], P('tp', 'ctx'), as said below
- block_output_gradient: bfloat16 [2048, 8192], P(('ctx', 'tp')), may hold values from -6 to 6
- w_out: bfloat16 [2048, 8192], P('tp'), may hold values from -0.125 to 0.125
- adapter_down_factor: bfloat16 [2048, 64], P('tp'), may hold values from -0.125 to 0.125
- adapter_up: bfloat16 [64, 8192], replicated, may hold values from -0.0625 to 0.0625
Outputs:
- grad_query: bfloat16 [2048, 2048], P('ctx', 'tp')
- grad_keys: bfloat16 [2048, 512], P('ctx', 'tp')
- grad_values: bfloat16 [2048, 512], P('ctx', 'tp')
- down_factor_gradient: float32 [2048, 64], P('tp')
- up_factor_gradient: bfloat16 [64, 8192], replicated
The draws below stay inside these ranges and needn't reach their ends.
Inputs may be any that keep to these rules, and one draw needn't show every extreme that they name: log_norm[h, r] minus the natural logarithm of (1 + pos(r)) lies between 0 and 1.5. `keys_copied`: for every g below 2, the 128 columns from 2 * g * 128 equal the 128 columns that follow them. `values_copied`: for every g below 2, the 128 columns from 2 * g * 128 equal the 128 columns that follow them.
All inputs are finite; a program needn't handle non-finite values.
Results may differ from the reference program's by a relative error of at most 0.022.
Values may be sent and summed in bfloat16 or wider, within the bound.
A program may use at most 64 MiB of HBM per device.

```python
import jax
import jax.numpy as jnp
from jax import lax

D = 8192
HD = 128
GROUP = 8
RANK = 64
TOK_DEV = 256
HEADS = 16
KVH = 2
TOKENS = 2048
N_CTX = 8


def copied_heads(key):
    normal_draw = jax.random.normal(key, (TOKENS, KVH, 1, HD), jnp.float32)
    normal_draw = jnp.clip(normal_draw, -6.0, 6.0)
    doubled = jnp.broadcast_to(normal_draw, (TOKENS, KVH, 2, HD))
    return doubled.reshape(TOKENS, 2 * KVH * HD)


def draw_keys_copied(key, part):
    key = jax.random.fold_in(key, 21)
    return copied_heads(key).astype(jnp.bfloat16)


def draw_values_copied(key, part):
    key = jax.random.fold_in(key, 37)
    return copied_heads(key).astype(jnp.bfloat16)


def draw_log_norm(key, part):
    key = jax.random.fold_in(key, 11)
    row_ids = jnp.arange(TOKENS, dtype=jnp.int32)
    device_count = TOKENS // TOK_DEV
    device = row_ids // TOK_DEV
    offset_rows = row_ids % TOK_DEV
    half_rows = TOK_DEV // 2
    early_pos = device * half_rows + offset_rows
    late_pos = (2 * device_count - 1 - device) * half_rows + offset_rows - half_rows
    positions = jnp.where(offset_rows < half_rows, early_pos, late_pos)
    baseline = jnp.log(positions.astype(jnp.float32) + 1.0)
    extra = jax.random.uniform(key, (HEADS, TOKENS), jnp.float32, 0.25, 1.0)
    return baseline[None, :] + extra


def steps_of(stream_key, extent, shards, smallest, largest):
    def one(axis_at, parts):
        draws = jax.random.uniform(jax.random.fold_in(jax.random.fold_in(stream_key, 6), axis_at), (parts,), jnp.float32, smallest / len(shards), largest / len(shards))
        return jnp.repeat(jnp.exp(draws), extent[axis_at] // parts).reshape((-1,) + (1,) * (len(extent) - axis_at - 1))

    loudness = one(*shards[0])
    for cut in shards[1:]:
        loudness = loudness * one(*cut)
    return loudness


def scatter_about(rng, shape, scale, limit, pieces=(), held_as=jnp.bfloat16):
    gain = steps_of(rng, shape, pieces, -0.22, 0.18) if pieces else 1.0
    drawn = jax.random.normal(rng, shape, jnp.float32) * scale * gain
    return jnp.minimum(jnp.maximum(drawn, -limit), limit).astype(held_as)


def setup_inputs(seed: int = 0) -> dict:
    keys = jax.random.split(jax.random.key(seed), 10)
    return {
        "queries": scatter_about(keys[0], (TOKENS, HEADS * HD), 1.0, 6.0, ((0, 8), (1, 4))),
        "keys_copied": draw_keys_copied(jax.random.fold_in(keys[9], 71), 0),
        "values_copied": draw_values_copied(jax.random.fold_in(keys[9], 71), 0),
        "attention_output_saved": scatter_about(keys[3], (TOKENS, HEADS * HD), 1.0, 6.0, ((0, 8), (1, 4))),
        "log_norm": draw_log_norm(jax.random.fold_in(keys[9], 71), 0),
        "block_output_gradient": scatter_about(keys[5], (TOKENS, D), 1.0, 6.0, ((0, 32),)),
        "w_out": scatter_about(keys[6], (HEADS * HD, D), (HEADS * HD) ** -0.5, 0.125, ((0, 4),)),
        "adapter_down_factor": scatter_about(keys[7], (HEADS * HD, RANK), (HEADS * HD) ** -0.5, 0.125, ((0, 4),)),
        "adapter_up": scatter_about(keys[8], (RANK, D), D ** -0.5, 0.0625),
    }


adapter_scale_factor = 2.0


def folded_positions():
    row_ids = jnp.arange(TOKENS, dtype=jnp.int32)
    device = row_ids // TOK_DEV
    offset_rows = row_ids % TOK_DEV
    half_rows = TOK_DEV // 2
    early_pos = device * half_rows + offset_rows
    late_pos = (2 * N_CTX - 1 - device) * half_rows + offset_rows - half_rows
    return jnp.where(offset_rows < half_rows, early_pos, late_pos)


def reference(queries, keys_copied, values_copied, attention_output_saved, log_norm, block_output_gradient, w_out, adapter_down_factor, adapter_up):
    adapter_cotangent_rows = jnp.dot(block_output_gradient, adapter_up.T, preferred_element_type=jnp.float32).astype(jnp.bfloat16)
    frozen_weight_gradient = jnp.dot(block_output_gradient, w_out.T, preferred_element_type=jnp.float32)
    adapter_input_gradient = jnp.dot(adapter_cotangent_rows, adapter_down_factor.T, preferred_element_type=jnp.float32)
    attention_output_gradient = (frozen_weight_gradient + adapter_scale_factor * adapter_input_gradient).astype(jnp.bfloat16)
    mixed_heads_rows = jnp.dot(attention_output_saved, adapter_down_factor, preferred_element_type=jnp.float32).astype(jnp.bfloat16)
    up_factor_gradient = (adapter_scale_factor * jnp.dot(mixed_heads_rows.T, block_output_gradient, preferred_element_type=jnp.float32)).astype(jnp.bfloat16)
    down_factor_gradient = adapter_scale_factor * jnp.dot(attention_output_saved.T, adapter_cotangent_rows, preferred_element_type=jnp.float32)
    product = attention_output_gradient.astype(jnp.float32) * attention_output_saved.astype(jnp.float32)
    row_delta = jnp.sum(product.reshape(TOKENS, HEADS, HD), axis=2)
    positions = folded_positions()
    visible = positions[:, None] >= positions[None, :]
    softmax_scale = HD ** -0.5
    half_group = GROUP // 2

    def one_group(group_index):
        def one_head(sums, member):
            head = group_index * GROUP + member
            column = (2 * group_index + member // half_group) * HD
            keys_head = lax.dynamic_slice_in_dim(keys_copied, column, HD, 1)
            values_head = lax.dynamic_slice_in_dim(values_copied, column, HD, 1)
            query_head = lax.dynamic_slice_in_dim(queries, head * HD, HD, 1)
            grad_head = lax.dynamic_slice_in_dim(attention_output_gradient, head * HD, HD, 1)
            norm_row = lax.dynamic_slice_in_dim(log_norm, head, 1, 0)[0]
            delta_row = lax.dynamic_slice_in_dim(row_delta, head, 1, 1)[:, 0]
            scores = jnp.dot(query_head, keys_head.T, preferred_element_type=jnp.float32) * softmax_scale
            attn_prob = jnp.where(visible, jnp.exp(scores - norm_row[:, None]), jnp.float32(0.0))
            probs_low = attn_prob.astype(jnp.bfloat16)
            value_grad = jnp.dot(probs_low.T, grad_head, preferred_element_type=jnp.float32)
            prob_grad = jnp.dot(grad_head, values_head.T, preferred_element_type=jnp.float32)
            score_grad = (attn_prob * (prob_grad - delta_row[:, None])).astype(jnp.bfloat16)
            query_grad = (jnp.dot(score_grad, keys_head, preferred_element_type=jnp.float32) * softmax_scale).astype(jnp.bfloat16)
            key_grad = jnp.dot(score_grad.T, query_head, preferred_element_type=jnp.float32) * softmax_scale
            return (sums[0] + key_grad, sums[1] + value_grad), query_grad

        zero_sums = (jnp.zeros((TOKENS, HD), jnp.float32), jnp.zeros((TOKENS, HD), jnp.float32))
        sums, query_grads = lax.scan(one_head, zero_sums, jnp.arange(GROUP, dtype=jnp.int32))
        return sums[0].astype(jnp.bfloat16), sums[1].astype(jnp.bfloat16), query_grads

    key_grads, value_grads, query_grads = lax.map(one_group, jnp.arange(KVH, dtype=jnp.int32))
    grad_query = jnp.transpose(query_grads, (2, 0, 1, 3)).reshape(TOKENS, HEADS * HD)
    key_twice = jnp.repeat(key_grads, 2, axis=0)
    value_twice = jnp.repeat(value_grads, 2, axis=0)
    grad_keys = jnp.transpose(key_twice, (1, 0, 2)).reshape(TOKENS, 2 * KVH * HD)
    grad_values = jnp.transpose(value_twice, (1, 0, 2)).reshape(TOKENS, 2 * KVH * HD)
    return grad_query, grad_keys, grad_values, down_factor_gradient, up_factor_gradient
```

```python
import functools

import jax
import jax.numpy as jnp
from jax import lax
from jax.experimental import pallas as pl
from jax.experimental.pallas import tpu as pltpu
from jax.sharding import PartitionSpec as P

adapter_scale_factor = 2.0
MESH = pl.DeviceIdType.MESH
F32 = jnp.float32
BF16 = jnp.bfloat16
NT = (((1,), (1,)), ((), ()))
TN = (((0,), (0,)), ((), ()))
CHUNKS = 4


def dot(a, b, dims=(((1,), (0,)), ((), ()))):
    return lax.dot_general(a, b, dims, preferred_element_type=F32)


def kernel(
    ctx_n, tp_n, heads,
    q_ref, k_ref, v_ref, ao_ref, ln_ref, g_hbm, w_hbm, down_ref, up_ref,
    dq_out, dk_out, dv_out, down_out, up_out,
    gath, w, dacc, down_pad,
    cot, mix_send, mix_recv,
    u_send, u_recv, uz, u_all,
    d_recv, kv, probs, q_st, do_st, ln_st, delta_st, dq_st,
    dkv_acc, dkv_send, dkv_recv, pair_buf,
    loc_sem, gr_s, gr_r, gl_s, gl_r,
    kv_s, kv_r, cot_s, cot_r, mix_s, mix_r, u_s, u_r, uz_s, uz_r, ua_s, ua_r,
    d_s, d_r, dkv_s, dkv_r, pair_s, pair_r,
):
    c = lax.axis_index("ctx")
    z = lax.axis_index("tp")
    rows = q_ref.shape[0]
    half = rows // 2
    blk = rows // tp_n
    width = g_hbm.shape[1]
    cw = width // CHUNKS
    uw = width // ctx_n
    rank = down_ref.shape[1]
    hd = q_ref.shape[1] // heads
    scale = hd ** (-0.5)
    cells = 2 * ctx_n

    w_copies = [
        pltpu.make_async_copy(
            w_hbm.at[:, pl.ds(i * cw, cw)], w.at[i], loc_sem.at[CHUNKS + i]
        )
        for i in range(CHUNKS)
    ]
    g_copies = [
        pltpu.make_async_copy(g_hbm.at[:, pl.ds(i * cw, cw)], gath.at[z, i], loc_sem.at[i])
        for i in range(CHUNKS)
    ]
    for cp in g_copies:
        cp.start()
    for cp in w_copies:
        cp.start()

    barrier = pltpu.get_barrier_semaphore()
    for k in range(1, ctx_n):
        pl.semaphore_signal(
            barrier, inc=1, device_id={"ctx": lax.rem(c + k, ctx_n), "tp": z}, device_id_type=MESH
        )
    for k in range(1, tp_n):
        pl.semaphore_signal(
            barrier, inc=1, device_id={"ctx": c, "tp": lax.rem(z + k, tp_n)}, device_id_type=MESH
        )
    pl.semaphore_wait(barrier, ctx_n - 1 + tp_n - 1)

    def ctx_copy(k, src, dst, s, r):
        return pltpu.make_async_remote_copy(
            src_ref=src, dst_ref=dst, send_sem=s.at[k], recv_sem=r.at[k],
            device_id={"ctx": lax.rem(c + k, ctx_n), "tp": z}, device_id_type=MESH,
        )

    def tp_copy(k, src, dst, s, r):
        return pltpu.make_async_remote_copy(
            src_ref=src, dst_ref=dst, send_sem=s.at[k], recv_sem=r.at[k],
            device_id={"ctx": c, "tp": lax.rem(z + k, tp_n)}, device_id_type=MESH,
        )

    def right_copy(s, i):
        return pltpu.make_async_remote_copy(
            src_ref=gath.at[z - s, i], dst_ref=gath.at[z - s, i],
            send_sem=gr_s.at[s, i], recv_sem=gr_r.at[s, i],
            device_id={"ctx": c, "tp": z + 1}, device_id_type=MESH,
        )

    def left_copy(s, i):
        return pltpu.make_async_remote_copy(
            src_ref=gath.at[z + s, i], dst_ref=gath.at[z + s, i],
            send_sem=gl_s.at[s, i], recv_sem=gl_r.at[s, i],
            device_id={"ctx": c, "tp": z - 1}, device_id_type=MESH,
        )

    def sends_right(s):
        return jnp.logical_and(z - s >= 0, z + 1 < tp_n)

    def sends_left(s):
        return jnp.logical_and(z + s < tp_n, z - 1 >= 0)

    for i in range(CHUNKS):
        g_copies[i].wait()

        @pl.when(sends_right(0))
        def _(i=i):
            right_copy(0, i).start()

        @pl.when(sends_left(0))
        def _(i=i):
            left_copy(0, i).start()

    kv[c, 0] = k_ref[...]
    kv[c, 1] = v_ref[...]
    kv_copies = [ctx_copy(k, kv.at[c], kv.at[c], kv_s, kv_r) for k in range(1, ctx_n)]
    for cp in kv_copies:
        cp.start()

    down_pad[...] = jnp.zeros_like(down_pad)
    down_pad[:, :rank] = down_ref[...]
    cot_own = jnp.zeros((blk, rank), F32)
    for i in range(CHUNKS):
        cot_own += dot(gath[z, i], up_ref[:, i * cw : (i + 1) * cw], NT)
    cot[z] = jnp.zeros((blk, cot.shape[2]), BF16)
    cot[z, :, :rank] = cot_own.astype(BF16)
    cot_copies = [tp_copy(k, cot.at[z], cot.at[z], cot_s, cot_r) for k in range(1, tp_n)]
    for cp in cot_copies:
        cp.start()
    mix_send[...] = dot(ao_ref[...], down_pad[...]).reshape(mix_send.shape)
    mix_copies = [
        tp_copy(k, mix_send.at[lax.rem(z + k, tp_n)], mix_recv.at[z], mix_s, mix_r)
        for k in range(1, tp_n)
    ]
    for cp in mix_copies:
        cp.start()
    mix_recv[z] = mix_send[z]

    for part in range(2):
        for h in range(heads):
            q_st[part, h * half : (h + 1) * half, :] = q_ref[
                part * half : (part + 1) * half, h * hd : (h + 1) * hd
            ]
            ln_st[part, :, h * half : (h + 1) * half] = ln_ref[
                h : h + 1, part * half : (part + 1) * half
            ]
    dq_st[...] = jnp.zeros_like(dq_st)
    dkv_acc[...] = jnp.zeros_like(dkv_acc)

    for cp in w_copies:
        cp.wait()

    def project(b, i):
        dacc[b] += dot(gath[b, i], w[i], NT)

    dacc[...] = jnp.zeros_like(dacc)
    for i in range(CHUNKS):
        project(z, i)

    def place(pair):
        early = pair <= c
        cell = jnp.where(early, pair, pair - c - 1)
        part = jnp.where(early, 0, 1)
        late_cell = cell >= ctx_n
        dev = jnp.where(late_cell, cells - 1 - cell, cell)
        start = pl.multiple_of(jnp.where(late_cell, half, 0), half)
        return early, cell, part, dev, start

    ctx_up_copies = [
        ctx_copy(k, u_send.at[lax.rem(c + k, ctx_n)], u_recv.at[c], u_s, u_r)
        for k in range(1, ctx_n)
    ]
    d_copies = [ctx_copy(k, d_recv.at[c], d_recv.at[c], d_s, d_r) for k in range(1, ctx_n)]
    uz_copies = [tp_copy(k, uz.at[z], uz.at[z], uz_s, uz_r) for k in range(1, tp_n)]
    ua_copies = [ctx_copy(k, u_all.at[c], u_all.at[c], ua_s, ua_r) for k in range(1, ctx_n)]

    def first_parts():
        for cp in mix_copies:
            cp.wait_recv()
        mixed = mix_recv[0]
        for t in range(1, tp_n):
            mixed += mix_recv[t]
        mixed = mixed.astype(BF16)
        for j in range(ctx_n):
            i, off = (j * uw) // cw, (j * uw) % cw
            part = dot(mixed, gath[z, i, :, off : off + uw], TN)
            u_send[j] = (adapter_scale_factor * part[:rank]).astype(BF16)
        for cp in ctx_up_copies:
            cp.start()
        u_recv[c] = u_send[c]
        for cp in cot_copies:
            cp.wait_recv()
        cot_rows = cot[...].reshape(rows, cot.shape[2])
        part = dot(cot_rows, ao_ref[...], TN)
        d_recv[c] = (adapter_scale_factor * part[:rank]).astype(BF16)
        for cp in d_copies:
            cp.start()

    def probabilities():
        for cp in kv_copies:
            cp.wait_recv()

        def body(pair, _):
            early, cell, part, dev, start = place(pair)
            keys = kv[dev, 0, pl.ds(start, half), :]
            scores = dot(keys, q_st[part], NT) * scale
            q_cell = jnp.where(early, c, cells - 1 - c)
            shape = (half, half)
            key_pos = cell * half + lax.broadcasted_iota(jnp.int32, shape, 0)
            q_pos = q_cell * half + lax.broadcasted_iota(jnp.int32, shape, 1)
            seen = q_pos >= key_pos
            for h in range(heads):
                cols = slice(h * half, (h + 1) * half)
                p = jnp.exp(scores[:, cols] - ln_st[part, :, cols])
                probs[pair, :, cols] = jnp.where(seen, p, 0.0)
            return 0

        lax.fori_loop(0, cells + 1, body, 0)

    def second_parts():
        for cp in ctx_up_copies:
            cp.wait_recv()
        total = u_recv[0].astype(F32)
        for j in range(1, ctx_n):
            total += u_recv[j].astype(F32)
        uz[z] = total.astype(BF16)
        for cp in uz_copies:
            cp.start()
        for cp in d_copies:
            cp.wait_recv()
        total = d_recv[0].astype(F32)
        for j in range(1, ctx_n):
            total += d_recv[j].astype(F32)
        down_out[...] = total

    def third_parts():
        for cp in uz_copies:
            cp.wait_recv()
        total = uz[0].astype(F32)
        for t in range(1, tp_n):
            total += uz[t].astype(F32)
        u_all[c] = total.astype(BF16)
        for cp in ua_copies:
            cp.start()

    for s in range(tp_n - 1):
        from_left = z - 1 - s >= 0
        from_right = z + 1 + s < tp_n
        for i in range(CHUNKS):
            @pl.when(from_left)
            def _(s=s, i=i):
                right_copy(s, i).wait_recv()

                @pl.when(z + 1 < tp_n)
                def _():
                    pltpu.make_async_remote_copy(
                        src_ref=gath.at[z - 1 - s, i], dst_ref=gath.at[z - 1 - s, i],
                        send_sem=gr_s.at[s + 1, i], recv_sem=gr_r.at[s + 1, i],
                        device_id={"ctx": c, "tp": z + 1}, device_id_type=MESH,
                    ).start()

                project(z - 1 - s, i)

            @pl.when(from_right)
            def _(s=s, i=i):
                left_copy(s, i).wait_recv()

                @pl.when(z - 1 >= 0)
                def _():
                    pltpu.make_async_remote_copy(
                        src_ref=gath.at[z + 1 + s, i], dst_ref=gath.at[z + 1 + s, i],
                        send_sem=gl_s.at[s + 1, i], recv_sem=gl_r.at[s + 1, i],
                        device_id={"ctx": c, "tp": z - 1}, device_id_type=MESH,
                    ).start()

                project(z + 1 + s, i)

            if s == 0 and i == 0:
                first_parts()
            if s == 0 and i == 2:
                probabilities()
            if s == 1 and i == 0:
                second_parts()
            if s == 1 and i == 2:
                third_parts()

    cot_rows = cot[...].reshape(rows, cot.shape[2])
    d_attn = dacc[...].reshape(rows, dacc.shape[2]) + adapter_scale_factor * dot(
        cot_rows, down_pad[...], NT
    )
    d_attn = d_attn.astype(BF16)
    for part in range(2):
        for h in range(heads):
            r0, c0 = part * half, h * hd
            block = d_attn[r0 : r0 + half, c0 : c0 + hd]
            do_st[part, h * half : (h + 1) * half, :] = block
            prod = block.astype(F32) * ao_ref[r0 : r0 + half, c0 : c0 + hd].astype(F32)
            delta_st[part, :, h * half : (h + 1) * half] = jnp.sum(prod.T, axis=0, keepdims=True)

    def backward(pair, _):
        early, cell, part, dev, start = place(pair)
        keys = kv[dev, 0, pl.ds(start, half), :]
        values = kv[dev, 1, pl.ds(start, half), :]
        p = probs[pair]
        grads = do_st[part]
        prob_grad = dot(values, grads, NT)
        score_grad = (p * (prob_grad - delta_st[part])).astype(BF16)
        dkv_acc[dev, 1, pl.ds(start, half), :] += dot(p.astype(BF16), grads)
        dkv_acc[dev, 0, pl.ds(start, half), :] += dot(score_grad, q_st[part])
        dq_st[part] += dot(score_grad, keys, TN)
        return 0

    lax.fori_loop(0, cells + 1, backward, 0)

    dkv_copies = [
        ctx_copy(k, dkv_send.at[lax.rem(c + k, ctx_n)], dkv_recv.at[c], dkv_s, dkv_r)
        for k in range(1, ctx_n)
    ]
    for k in list(range(1, ctx_n)):
        j = lax.rem(c + k, ctx_n)
        dkv_send[j, 0] = (dkv_acc[j, 0] * scale).astype(BF16)
        dkv_send[j, 1] = dkv_acc[j, 1].astype(BF16)
        dkv_copies[k - 1].start()
    dkv_recv[c, 0] = (dkv_acc[c, 0] * scale).astype(BF16)
    dkv_recv[c, 1] = dkv_acc[c, 1].astype(BF16)

    for part in range(2):
        for h in range(heads):
            dq_out[part * half : (part + 1) * half, h * hd : (h + 1) * hd] = (
                dq_st[part, h * half : (h + 1) * half, :] * scale
            ).astype(BF16)
    for cp in ua_copies:
        cp.wait_recv()
    for j in range(ctx_n):
        up_out[:, j * uw : (j + 1) * uw] = u_all[j]

    for cp in dkv_copies:
        cp.wait_recv()
    total = dkv_recv[0].astype(F32)
    for j in range(1, ctx_n):
        total += dkv_recv[j].astype(F32)
    pair_buf[0] = total.astype(BF16)
    other = z + 1 - 2 * lax.rem(z, 2)
    pair_copy = pltpu.make_async_remote_copy(
        src_ref=pair_buf.at[0], dst_ref=pair_buf.at[1], send_sem=pair_s, recv_sem=pair_r,
        device_id={"ctx": c, "tp": other}, device_id_type=MESH,
    )
    pair_copy.start()
    pair_copy.wait_recv()
    sums = pair_buf[0].astype(F32) + pair_buf[1].astype(F32)
    dk_out[...] = sums[0].astype(BF16)
    dv_out[...] = sums[1].astype(BF16)

    for group in (
        kv_copies, cot_copies, mix_copies, ctx_up_copies, d_copies, uz_copies, ua_copies, dkv_copies
    ):
        for cp in group:
            cp.wait_send()
    pair_copy.wait_send()
    for s in range(tp_n - 1):
        for i in range(CHUNKS):
            @pl.when(sends_right(s))
            def _(s=s, i=i):
                right_copy(s, i).wait_send()

            @pl.when(sends_left(s))
            def _(s=s, i=i):
                left_copy(s, i).wait_send()


def local(q, k, v, ao, ln, g, w, down, up):
    ctx_n = lax.axis_size("ctx")
    tp_n = lax.axis_size("tp")
    rows, q_cols = q.shape
    heads = ln.shape[0]
    hd = q_cols // heads
    half = rows // 2
    blk = rows // tp_n
    width = g.shape[1]
    cw = width // CHUNKS
    uw = width // ctx_n
    proj = w.shape[0]
    rank = down.shape[1]
    lanes = max(128, rank)
    pairs = 2 * ctx_n + 1
    vmem = pl.BlockSpec(memory_space=pltpu.VMEM)
    hbm = pl.BlockSpec(memory_space=pl.ANY)
    V = pltpu.VMEM
    DMA = pltpu.SemaphoreType.DMA
    scratch = [
        V((tp_n, CHUNKS, blk, cw), BF16),
        V((CHUNKS, proj, cw), BF16),
        V((tp_n, blk, proj), F32),
        V((proj, lanes), BF16),
        V((tp_n, blk, lanes), BF16),
        V((tp_n, blk, lanes), F32),
        V((tp_n, blk, lanes), F32),
        V((ctx_n, rank, uw), BF16),
        V((ctx_n, rank, uw), BF16),
        V((tp_n, rank, uw), BF16),
        V((ctx_n, rank, uw), BF16),
        V((ctx_n, rank, proj), BF16),
        V((ctx_n, 2, rows, hd), BF16),
        V((pairs, half, heads * half), F32),
        V((2, heads * half, hd), BF16),
        V((2, heads * half, hd), BF16),
        V((2, 1, heads * half), F32),
        V((2, 1, heads * half), F32),
        V((2, heads * half, hd), F32),
        V((ctx_n, 2, rows, hd), F32),
        V((ctx_n, 2, rows, hd), BF16),
        V((ctx_n, 2, rows, hd), BF16),
        V((2, 2, rows, hd), BF16),
        DMA((2 * CHUNKS,)),
    ]
    scratch += [DMA((tp_n, CHUNKS))] * 4
    scratch += [DMA((ctx_n,))] * 2 + [DMA((tp_n,))] * 4 + [DMA((ctx_n,))] * 2
    scratch += [DMA((tp_n,))] * 2 + [DMA((ctx_n,))] * 6 + [DMA, DMA]
    dq, dk, dv, dd, du = pl.pallas_call(
        functools.partial(kernel, ctx_n, tp_n, heads),
        out_shape=(
            jax.ShapeDtypeStruct(q.shape, BF16),
            jax.ShapeDtypeStruct(k.shape, BF16),
            jax.ShapeDtypeStruct(v.shape, BF16),
            jax.ShapeDtypeStruct((rank, proj), F32),
            jax.ShapeDtypeStruct(up.shape, BF16),
        ),
        in_specs=[vmem] * 5 + [hbm] * 2 + [vmem] * 2,
        out_specs=(vmem,) * 5,
        scratch_shapes=scratch,
        compiler_params=pltpu.CompilerParams(
            collective_id=0, has_side_effects=True, vmem_limit_bytes=60 * 2**20
        ),
        cost_estimate=pl.CostEstimate(
            flops=5 * 10**9, bytes_accessed=16 * 2**20, transcendentals=2**21
        ),
    )(q, k, v, ao, ln, g, w, down, up)
    return dq, dk, dv, dd.T, du


def solution(mesh):
    placed = (
        P("ctx", "tp"),
        P("ctx", "tp"),
        P("ctx", "tp"),
        P("ctx", "tp"),
        P("tp", "ctx"),
        P(("ctx", "tp"), None),
        P("tp", None),
        P("tp", None),
        P(),
    )
    return jax.shard_map(
        local,
        mesh=mesh,
        in_specs=placed,
        out_specs=(P("ctx", "tp"), P("ctx", "tp"), P("ctx", "tp"), P("tp", None), P()),
        check_vma=False,
    )
```

```python
import functools

import jax
import jax.numpy as jnp
from jax import lax
from jax.experimental import pallas as pl
from jax.experimental.pallas import tpu as pltpu
from jax.sharding import PartitionSpec as P

adapter_scale_factor = 2.0
MESH = pl.DeviceIdType.MESH
F32 = jnp.float32
BF16 = jnp.bfloat16
NT = (((1,), (1,)), ((), ()))
TN = (((0,), (0,)), ((), ()))
CHUNKS = 8
MOVED = 3
KEPT = CHUNKS - MOVED


def dot(a, b, dims=(((1,), (0,)), ((), ()))):
    return lax.dot_general(a, b, dims, preferred_element_type=F32)


def kernel(
    ctx_n, tp_n, heads,
    q_ref, k_ref, v_ref, ao_ref, ln_ref, g_hbm, w_hbm, down_ref, up_ref,
    dq_out, dk_out, dv_out, down_out, up_out,
    gath, w, dacc, down_pad,
    cot, mix_send, mix_recv,
    u_send, u_recv, u_sum, uz, uc, u_all, wx, px_send, px_recv,
    d_recv, kv, probs, q_st, do_st, ln_st, delta_st, dq_st,
    dkv_acc, dkv_send, dkv_recv, pair_buf,
    loc_sem, gr_s, gr_r, gl_s, gl_r,
    kv_s, kv_r, cot_s, cot_r, mix_s, mix_r, u_s, u_r, uz_s, uz_r, uc_s, uc_r, ua_s, ua_r,
    d_s, d_r, dkv_s, dkv_r, px_s, px_r, wa_s, wa_r, wf_s, wf_r, we_s, we_r, pair_s, pair_r,
):
    c = lax.axis_index("ctx")
    z = lax.axis_index("tp")
    rows = q_ref.shape[0]
    half = rows // 2
    blk = rows // tp_n
    width = g_hbm.shape[1]
    cw = width // CHUNKS
    uw = width // ctx_n
    rank = down_ref.shape[0]
    hd = q_ref.shape[1] // heads
    scale = hd ** (-0.5)
    cells = 2 * ctx_n

    w_copies = [
        pltpu.make_async_copy(
            w_hbm.at[:, pl.ds(i * cw, cw)], w.at[i], loc_sem.at[CHUNKS + i]
        )
        for i in range(CHUNKS)
    ]
    g_copies = [
        pltpu.make_async_copy(g_hbm.at[:, pl.ds(i * cw, cw)], gath.at[z, i], loc_sem.at[i])
        for i in range(CHUNKS)
    ]
    for cp in g_copies:
        cp.start()
    for cp in w_copies:
        cp.start()

    barrier = pltpu.get_barrier_semaphore()
    for k in range(1, ctx_n):
        pl.semaphore_signal(
            barrier, inc=1, device_id={"ctx": lax.rem(c + k, ctx_n), "tp": z}, device_id_type=MESH
        )
    for k in range(1, tp_n):
        pl.semaphore_signal(
            barrier, inc=1, device_id={"ctx": c, "tp": lax.rem(z + k, tp_n)}, device_id_type=MESH
        )
    pl.semaphore_wait(barrier, ctx_n - 1 + tp_n - 1)

    def ctx_copy(k, src, dst, s, r):
        return pltpu.make_async_remote_copy(
            src_ref=src, dst_ref=dst, send_sem=s.at[k], recv_sem=r.at[k],
            device_id={"ctx": lax.rem(c + k, ctx_n), "tp": z}, device_id_type=MESH,
        )

    def tp_copy(k, src, dst, s, r):
        return pltpu.make_async_remote_copy(
            src_ref=src, dst_ref=dst, send_sem=s.at[k], recv_sem=r.at[k],
            device_id={"ctx": c, "tp": lax.rem(z + k, tp_n)}, device_id_type=MESH,
        )

    def right_copy(s, i):
        return pltpu.make_async_remote_copy(
            src_ref=gath.at[z - s, i], dst_ref=gath.at[z - s, i],
            send_sem=gr_s.at[s, i], recv_sem=gr_r.at[s, i],
            device_id={"ctx": c, "tp": z + 1}, device_id_type=MESH,
        )

    def left_copy(s, i):
        return pltpu.make_async_remote_copy(
            src_ref=gath.at[z + s, i], dst_ref=gath.at[z + s, i],
            send_sem=gl_s.at[s, i], recv_sem=gl_r.at[s, i],
            device_id={"ctx": c, "tp": z - 1}, device_id_type=MESH,
        )

    def sends_right(s, i):
        last = tp_n - 1 if i >= kept else tp_n
        return jnp.logical_and(z - s >= 0, z + 1 < last)

    def sends_left(s, i):
        first = 1 if i >= kept else 0
        return jnp.logical_and(z + s < tp_n, z - 1 >= first)

    moved = moved_chunks(tp_n)
    kept = CHUNKS - moved
    proj = w_hbm.shape[0]
    wr = proj // ctx_n
    is_edge = jnp.logical_or(z == 0, z == tp_n - 1)
    is_helper = jnp.logical_or(z == 1, z == tp_n - 2)
    inward = jnp.where(z == 0, 1, -1)
    beyond = jnp.where(z == 1, 1, -1)

    def wx_rows(j):
        return wx.at[:, pl.ds(pl.multiple_of(j * wr, wr), wr), :]

    edge_copy = None
    if moved:
        edge_copy = pltpu.make_async_remote_copy(
            src_ref=w.at[pl.ds(kept, moved), pl.ds(pl.multiple_of(c * wr, wr), wr), :],
            dst_ref=wx_rows(c), send_sem=we_s, recv_sem=we_r,
            device_id={"ctx": c, "tp": z + inward}, device_id_type=MESH,
        )

        @pl.when(is_edge)
        def _():
            for cp in w_copies:
                cp.wait()
            edge_copy.start()

        @pl.when(jnp.logical_not(is_edge))
        def _():
            for cp in w_copies:
                cp.wait()
    else:
        for cp in w_copies:
            cp.wait()

    for i in range(CHUNKS):
        g_copies[i].wait()

        @pl.when(sends_right(0, i))
        def _(i=i):
            right_copy(0, i).start()

        @pl.when(sends_left(0, i))
        def _(i=i):
            left_copy(0, i).start()

    kv[c, 0] = k_ref[...]
    kv[c, 1] = v_ref[...]
    kv_copies = [ctx_copy(k, kv.at[c], kv.at[c], kv_s, kv_r) for k in range(1, ctx_n)]
    for cp in kv_copies:
        cp.start()

    down_pad[...] = jnp.zeros_like(down_pad)
    down_pad[:rank, :] = down_ref[...]
    cot_own = jnp.zeros((blk, rank), F32)
    for i in range(CHUNKS):
        cot_own += dot(gath[z, i], up_ref[:, i * cw : (i + 1) * cw], NT)
    cot[z] = jnp.zeros((blk, cot.shape[2]), BF16)
    cot[z, :, :rank] = cot_own.astype(BF16)
    cot_copies = [tp_copy(k, cot.at[z], cot.at[z], cot_s, cot_r) for k in range(1, tp_n)]
    for cp in cot_copies:
        cp.start()
    mix_send[...] = dot(ao_ref[...], down_pad[...], NT).reshape(mix_send.shape)
    mix_copies = [
        tp_copy(k, mix_send.at[lax.rem(z + k, tp_n)], mix_recv.at[z], mix_s, mix_r)
        for k in range(1, tp_n)
    ]
    for cp in mix_copies:
        cp.start()
    mix_recv[z] = mix_send[z]

    for part in range(2):
        for h in range(heads):
            q_st[part, h * half : (h + 1) * half, :] = q_ref[
                part * half : (part + 1) * half, h * hd : (h + 1) * hd
            ]
            ln_st[part, :, h * half : (h + 1) * half] = ln_ref[
                h : h + 1, part * half : (part + 1) * half
            ]
    dq_st[...] = jnp.zeros_like(dq_st)
    dkv_acc[...] = jnp.zeros_like(dkv_acc)

    def project(b, i):
        dacc[b] += dot(gath[b, i], w[i], NT)

    dacc[...] = jnp.zeros_like(dacc)
    for i in range(CHUNKS):
        project(z, i)

    def place(pair):
        early = pair <= c
        cell = jnp.where(early, pair, pair - c - 1)
        part = jnp.where(early, 0, 1)
        late_cell = cell >= ctx_n
        dev = jnp.where(late_cell, cells - 1 - cell, cell)
        start = pl.multiple_of(jnp.where(late_cell, half, 0), half)
        return early, cell, part, dev, start

    ctx_up_copies = [
        ctx_copy(k, u_send.at[lax.rem(c + k, ctx_n)], u_recv.at[c], u_s, u_r)
        for k in range(1, ctx_n)
    ]
    d_copies = [ctx_copy(k, d_recv.at[c], d_recv.at[c], d_s, d_r) for k in range(1, ctx_n)]
    rq = uz.shape[1]
    scattered = rq < rank

    def u_rows(t):
        return u_sum.at[pl.ds(pl.multiple_of(t * rq, rq), rq), :] if scattered else u_sum

    uz_copies = [
        tp_copy(k, u_rows(lax.rem(z + k, tp_n)), uz.at[z], uz_s, uz_r) for k in range(1, tp_n)
    ]
    uc_copies = []
    if scattered:
        uc_copies = [tp_copy(k, uc.at[z], uc.at[z], uc_s, uc_r) for k in range(1, tp_n)]
    ua_copies = [ctx_copy(k, u_all.at[c], u_all.at[c], ua_s, ua_r) for k in range(1, ctx_n)]

    def first_parts():
        for cp in mix_copies:
            cp.wait_recv()
        mixed = mix_recv[0]
        for t in range(1, tp_n):
            mixed += mix_recv[t]
        mixed = mixed.astype(BF16)
        for j in range(ctx_n):
            i, off = (j * uw) // cw, (j * uw) % cw
            part = dot(mixed, gath[z, i, :, off : off + uw], TN)
            u_send[j] = (adapter_scale_factor * part[:rank]).astype(BF16)
        for cp in ctx_up_copies:
            cp.start()
        u_recv[c] = u_send[c]
        for cp in cot_copies:
            cp.wait_recv()
        cot_rows = cot[...].reshape(rows, cot.shape[2])
        part = dot(cot_rows, ao_ref[...], TN)
        d_recv[c] = (adapter_scale_factor * part[:rank]).astype(BF16)
        for cp in d_copies:
            cp.start()

    def probabilities():
        for cp in kv_copies:
            cp.wait_recv()

        def body(pair, _):
            early, cell, part, dev, start = place(pair)
            keys = kv[dev, 0, pl.ds(start, half), :]
            scores = dot(keys, q_st[part], NT) * scale
            q_cell = jnp.where(early, c, cells - 1 - c)
            shape = (half, half)
            key_pos = cell * half + lax.broadcasted_iota(jnp.int32, shape, 0)
            q_pos = q_cell * half + lax.broadcasted_iota(jnp.int32, shape, 1)
            seen = q_pos >= key_pos
            for h in range(heads):
                cols = slice(h * half, (h + 1) * half)
                p = jnp.exp(scores[:, cols] - ln_st[part, :, cols])
                probs[pair, :, cols] = jnp.where(seen, p, 0.0)
            return 0

        lax.fori_loop(0, cells + 1, body, 0)

    def second_parts():
        for cp in ctx_up_copies:
            cp.wait_recv()
        total = u_recv[0].astype(F32)
        for j in range(1, ctx_n):
            total += u_recv[j].astype(F32)
        u_sum[...] = total.astype(BF16)
        for cp in uz_copies:
            cp.start()
        uz[z] = u_rows(z)[...]
        for cp in d_copies:
            cp.wait_recv()
        total = d_recv[0].astype(F32)
        for j in range(1, ctx_n):
            total += d_recv[j].astype(F32)
        down_out[...] = total

    def third_parts():
        for cp in uz_copies:
            cp.wait_recv()
        total = uz[0].astype(F32)
        for t in range(1, tp_n):
            total += uz[t].astype(F32)
        if scattered:
            uc[z] = total.astype(BF16)
            for cp in uc_copies:
                cp.start()
        else:
            u_all[c] = total.astype(BF16)

    def fourth_parts():
        if scattered:
            for cp in uc_copies:
                cp.wait_recv()
            u_all[c] = uc[...].reshape(u_all.shape[1:])
        for cp in ua_copies:
            cp.start()

    sibling = c + 1 - 2 * lax.rem(c, 2)
    own_rows = wx_rows(c) if moved else None
    wa_copies, wf_copies = [], []
    if moved:
        wa_copies = [
            ctx_copy(2 * k, own_rows, own_rows, wa_s, wa_r) for k in range(1, ctx_n // 2)
        ]
        for k in range(ctx_n // 2):
            block = wx_rows(lax.rem(c + ctx_n - 2 * k, ctx_n))
            wf_copies.append(
                pltpu.make_async_remote_copy(
                    src_ref=block, dst_ref=block, send_sem=wf_s.at[k], recv_sem=wf_r.at[k],
                    device_id={"ctx": sibling, "tp": z}, device_id_type=MESH,
                )
            )

    def px_copy(d):
        return pltpu.make_async_remote_copy(
            src_ref=px_send.at[d], dst_ref=px_recv.at[d], send_sem=px_s.at[d],
            recv_sem=px_r.at[d], device_id={"ctx": c, "tp": z - beyond}, device_id_type=MESH,
        )

    def weight_in():
        if moved:
            @pl.when(is_helper)
            def _():
                edge_copy.wait_recv()
                for cp in wa_copies:
                    cp.start()
                wf_copies[0].start()

    def weight_on():
        if moved:
            @pl.when(is_helper)
            def _():
                for k in range(1, ctx_n // 2):
                    wa_copies[k - 1].wait_recv()
                    wf_copies[k].start()

    def weight_whole():
        if moved:
            @pl.when(is_helper)
            def _():
                for cp in wf_copies:
                    cp.wait_recv()

    def help_with(d):
        if moved and d <= tp_n - 2:
            @pl.when(is_helper)
            def _():
                b = z + d * beyond
                part = dot(gath[b, kept], wx[0], NT)
                for i in range(1, moved):
                    part += dot(gath[b, kept + i], wx[i], NT)
                px_send[d] = part.astype(BF16)
                px_copy(d).start()

    for s in range(tp_n - 1):
        from_left = z - 1 - s >= 0
        from_right = z + 1 + s < tp_n
        for i in range(CHUNKS):
            @pl.when(jnp.logical_and(from_left, z < (tp_n - 1 if i >= kept else tp_n)))
            def _(s=s, i=i):
                right_copy(s, i).wait_recv()

                @pl.when(z + 1 < (tp_n - 1 if i >= kept else tp_n))
                def _():
                    pltpu.make_async_remote_copy(
                        src_ref=gath.at[z - 1 - s, i], dst_ref=gath.at[z - 1 - s, i],
                        send_sem=gr_s.at[s + 1, i], recv_sem=gr_r.at[s + 1, i],
                        device_id={"ctx": c, "tp": z + 1}, device_id_type=MESH,
                    ).start()

                project(z - 1 - s, i)

            @pl.when(jnp.logical_and(from_right, z > (0 if i >= kept else -1)))
            def _(s=s, i=i):
                left_copy(s, i).wait_recv()

                @pl.when(z - 1 >= (1 if i >= kept else 0))
                def _():
                    pltpu.make_async_remote_copy(
                        src_ref=gath.at[z + 1 + s, i], dst_ref=gath.at[z + 1 + s, i],
                        send_sem=gl_s.at[s + 1, i], recv_sem=gl_r.at[s + 1, i],
                        device_id={"ctx": c, "tp": z - 1}, device_id_type=MESH,
                    ).start()

                project(z + 1 + s, i)

            if s == 0 and i == 0:
                first_parts()
            if s == 0 and i == 2:
                weight_in()
            if s == 0 and i == 4:
                probabilities()
            if s == 1 and i == 0:
                weight_on()
                second_parts()
            if s == 1 and i == 2:
                third_parts()
                weight_whole()
                help_with(0)
                help_with(1)
            if s == 1 and i == 5:
                fourth_parts()
            if s >= 1 and i == CHUNKS - 1:
                help_with(s + 1)

    if moved:
        @pl.when(is_edge)
        def _():
            for d in range(tp_n - 1):
                b = z + (d + 1) * inward
                pltpu.make_async_remote_copy(
                    src_ref=px_send.at[d], dst_ref=px_recv.at[d], send_sem=px_s.at[d],
                    recv_sem=px_r.at[d], device_id={"ctx": c, "tp": z + inward},
                    device_id_type=MESH,
                ).wait_recv()
                dacc[b] += px_recv[d].astype(F32)

    cot_rows = cot[...].reshape(rows, cot.shape[2])
    d_attn = dacc[...].reshape(rows, dacc.shape[2]) + adapter_scale_factor * dot(
        cot_rows, down_pad[...]
    )
    d_attn = d_attn.astype(BF16)
    for part in range(2):
        for h in range(heads):
            r0, c0 = part * half, h * hd
            block = d_attn[r0 : r0 + half, c0 : c0 + hd]
            do_st[part, h * half : (h + 1) * half, :] = block
            prod = block.astype(F32) * ao_ref[r0 : r0 + half, c0 : c0 + hd].astype(F32)
            delta_st[part, :, h * half : (h + 1) * half] = jnp.sum(prod.T, axis=0, keepdims=True)

    def backward(pair, _):
        early, cell, part, dev, start = place(pair)
        keys = kv[dev, 0, pl.ds(start, half), :]
        values = kv[dev, 1, pl.ds(start, half), :]
        p = probs[pair]
        grads = do_st[part]
        prob_grad = dot(values, grads, NT)
        score_grad = (p * (prob_grad - delta_st[part])).astype(BF16)
        dkv_acc[dev, 1, pl.ds(start, half), :] += dot(p.astype(BF16), grads)
        dkv_acc[dev, 0, pl.ds(start, half), :] += dot(score_grad, q_st[part])
        dq_st[part] += dot(score_grad, keys, TN)
        return 0

    lax.fori_loop(0, cells + 1, backward, 0)

    dkv_copies = [
        ctx_copy(k, dkv_send.at[lax.rem(c + k, ctx_n)], dkv_recv.at[c], dkv_s, dkv_r)
        for k in range(1, ctx_n)
    ]
    for k in list(range(1, ctx_n)):
        j = lax.rem(c + k, ctx_n)
        dkv_send[j, 0] = (dkv_acc[j, 0] * scale).astype(BF16)
        dkv_send[j, 1] = dkv_acc[j, 1].astype(BF16)
        dkv_copies[k - 1].start()
    dkv_recv[c, 0] = (dkv_acc[c, 0] * scale).astype(BF16)
    dkv_recv[c, 1] = dkv_acc[c, 1].astype(BF16)

    for part in range(2):
        for h in range(heads):
            dq_out[part * half : (part + 1) * half, h * hd : (h + 1) * hd] = (
                dq_st[part, h * half : (h + 1) * half, :] * scale
            ).astype(BF16)
    for cp in ua_copies:
        cp.wait_recv()
    for j in range(ctx_n):
        up_out[:, j * uw : (j + 1) * uw] = u_all[j]

    for cp in dkv_copies:
        cp.wait_recv()
    total = dkv_recv[0].astype(F32)
    for j in range(1, ctx_n):
        total += dkv_recv[j].astype(F32)
    pair_buf[0] = total.astype(BF16)
    other = z + 1 - 2 * lax.rem(z, 2)
    pair_copy = pltpu.make_async_remote_copy(
        src_ref=pair_buf.at[0], dst_ref=pair_buf.at[1], send_sem=pair_s, recv_sem=pair_r,
        device_id={"ctx": c, "tp": other}, device_id_type=MESH,
    )
    pair_copy.start()
    pair_copy.wait_recv()
    sums = pair_buf[0].astype(F32) + pair_buf[1].astype(F32)
    dk_out[...] = sums[0].astype(BF16)
    dv_out[...] = sums[1].astype(BF16)

    for group in (
        kv_copies, cot_copies, mix_copies, ctx_up_copies, d_copies, uz_copies, uc_copies,
        ua_copies, dkv_copies,
    ):
        for cp in group:
            cp.wait_send()
    pair_copy.wait_send()
    if moved:
        @pl.when(is_edge)
        def _():
            edge_copy.wait_send()

        @pl.when(is_helper)
        def _():
            for cp in wa_copies + wf_copies:
                cp.wait_send()
            for d in range(tp_n - 1):
                px_copy(d).wait_send()
    for s in range(tp_n - 1):
        for i in range(CHUNKS):
            @pl.when(sends_right(s, i))
            def _(s=s, i=i):
                right_copy(s, i).wait_send()

            @pl.when(sends_left(s, i))
            def _(s=s, i=i):
                left_copy(s, i).wait_send()


def moved_chunks(tp_n):
    return MOVED if tp_n == 4 else 0


def hand_on(*refs):
    n = len(refs) // 2
    sems = refs[-1]
    copies = [pltpu.make_async_copy(refs[i], refs[n + i], sems.at[i]) for i in range(n)]
    for cp in copies:
        cp.start()
    for cp in copies:
        cp.wait()


def handed_on(*arrays):
    hbm = pl.BlockSpec(memory_space=pl.ANY)
    return pl.pallas_call(
        hand_on,
        out_shape=tuple(jax.ShapeDtypeStruct(a.shape, a.dtype) for a in arrays),
        in_specs=[hbm] * len(arrays),
        out_specs=(hbm,) * len(arrays),
        scratch_shapes=[pltpu.SemaphoreType.DMA((len(arrays),))],
    )(*arrays)


def local(q, k, v, ao, ln, g, w, down, up):
    ctx_n = lax.axis_size("ctx")
    tp_n = lax.axis_size("tp")
    rows, q_cols = q.shape
    heads = ln.shape[0]
    hd = q_cols // heads
    half = rows // 2
    blk = rows // tp_n
    width = g.shape[1]
    cw = width // CHUNKS
    uw = width // ctx_n
    proj = w.shape[0]
    rank = down.shape[1]
    moves = moved_chunks(tp_n) > 0
    rq = rank // tp_n if rank % (16 * tp_n) == 0 else rank
    lanes = max(128, rank)
    pairs = 2 * ctx_n + 1
    vmem = pl.BlockSpec(memory_space=pltpu.VMEM)
    hbm = pl.BlockSpec(memory_space=pl.ANY)
    V = pltpu.VMEM
    DMA = pltpu.SemaphoreType.DMA
    scratch = [
        V((tp_n, CHUNKS, blk, cw), BF16),
        V((CHUNKS, proj, cw), BF16),
        V((tp_n, blk, proj), F32),
        V((lanes, proj), BF16),
        V((tp_n, blk, lanes), BF16),
        V((tp_n, blk, lanes), F32),
        V((tp_n, blk, lanes), F32),
        V((ctx_n, rank, uw), BF16),
        V((ctx_n, rank, uw), BF16),
        V((rank, uw), BF16),
        V((tp_n, rq, uw), BF16),
        V((tp_n, rq, uw), BF16),
        V((ctx_n, rank, uw), BF16),
        V((MOVED, proj, cw) if moves else (1, 16, 128), BF16),
        V((tp_n, blk, proj) if moves else (1, 16, 128), BF16),
        V((tp_n, blk, proj) if moves else (1, 16, 128), BF16),
        V((ctx_n, rank, proj), BF16),
        V((ctx_n, 2, rows, hd), BF16),
        V((pairs, half, heads * half), F32),
        V((2, heads * half, hd), BF16),
        V((2, heads * half, hd), BF16),
        V((2, 1, heads * half), F32),
        V((2, 1, heads * half), F32),
        V((2, heads * half, hd), F32),
        V((ctx_n, 2, rows, hd), F32),
        V((ctx_n, 2, rows, hd), BF16),
        V((ctx_n, 2, rows, hd), BF16),
        V((2, 2, rows, hd), BF16),
        DMA((2 * CHUNKS,)),
    ]
    scratch += [DMA((tp_n, CHUNKS))] * 4
    scratch += [DMA((ctx_n,))] * 2 + [DMA((tp_n,))] * 4 + [DMA((ctx_n,))] * 2
    scratch += [DMA((tp_n,))] * 4 + [DMA((ctx_n,))] * 6 + [DMA((tp_n,))] * 2
    scratch += [DMA((ctx_n,))] * 4 + [DMA] * 4
    dq, dk, dv, dd, du = pl.pallas_call(
        functools.partial(kernel, ctx_n, tp_n, heads),
        out_shape=(
            jax.ShapeDtypeStruct(q.shape, BF16),
            jax.ShapeDtypeStruct(k.shape, BF16),
            jax.ShapeDtypeStruct(v.shape, BF16),
            jax.ShapeDtypeStruct((rank, proj), F32),
            jax.ShapeDtypeStruct(up.shape, BF16),
        ),
        in_specs=[vmem] * 5 + [hbm] * 2 + [vmem] * 2,
        out_specs=(vmem,) * 5,
        scratch_shapes=scratch,
        compiler_params=pltpu.CompilerParams(
            collective_id=0, has_side_effects=True, vmem_limit_bytes=60 * 2**20
        ),
        cost_estimate=pl.CostEstimate(
            flops=5 * 10**9, bytes_accessed=16 * 2**20, transcendentals=2**21
        ),
    )(q, k, v, ao, ln, g, w, down.T, up)
    dq, dk, dv, dd, du = handed_on(dq, dk, dv, dd, du)
    return dq, dk, dv, dd.T, du


def solution(mesh):
    placed = (
        P("ctx", "tp"),
        P("ctx", "tp"),
        P("ctx", "tp"),
        P("ctx", "tp"),
        P("tp", "ctx"),
        P(("ctx", "tp"), None),
        P("tp", None),
        P("tp", None),
        P(),
    )
    return jax.shard_map(
        local,
        mesh=mesh,
        in_specs=placed,
        out_specs=(P("ctx", "tp"), P("ctx", "tp"), P("ctx", "tp"), P("tp", None), P()),
        check_vma=False,
    )
```

```python
import functools

import jax
import jax.numpy as jnp
from jax import lax
from jax.experimental import pallas as pl
from jax.experimental.pallas import tpu as pltpu
from jax.sharding import PartitionSpec as P

adapter_scale_factor = 2.0
MESH = pl.DeviceIdType.MESH
F32 = jnp.float32
BF16 = jnp.bfloat16
NT = (((1,), (1,)), ((), ()))
TN = (((0,), (0,)), ((), ()))
CHUNKS = 8
MOVED = 3
KEPT = CHUNKS - MOVED


def dot(a, b, dims=(((1,), (0,)), ((), ()))):
    return lax.dot_general(a, b, dims, preferred_element_type=F32)


def kernel(
    ctx_n, tp_n, heads,
    q_ref, k_ref, v_ref, ao_ref, ln_ref, g_hbm, w_hbm, down_ref, up_ref,
    dq_out, dk_out, dv_out, down_out, up_out,
    gath, w, dacc, down_pad,
    cot, mix_send, mix_recv,
    u_send, u_recv, u_sum, uz, uc, u_all, wx, px_send, px_recv,
    d_recv, kv, probs, q_st, do_st, ln_st, delta_st, dq_st,
    dkv_acc, dkv_send, dkv_recv, pair_buf,
    loc_sem, gr_s, gr_r, gl_s, gl_r,
    kv_s, kv_r, cot_s, cot_r, mix_s, mix_r, u_s, u_r, uz_s, uz_r, uc_s, uc_r, ua_s, ua_r,
    d_s, d_r, dkv_s, dkv_r, px_s, px_r, wa_s, wa_r, wf_s, wf_r, we_s, we_r, pair_s, pair_r,
):
    c = lax.axis_index("ctx")
    z = lax.axis_index("tp")
    rows = q_ref.shape[0]
    half = rows // 2
    blk = rows // tp_n
    width = g_hbm.shape[1]
    cw = width // CHUNKS
    uw = width // ctx_n
    rank = down_ref.shape[0]
    hd = q_ref.shape[1] // heads
    scale = hd ** (-0.5)
    cells = 2 * ctx_n

    w_copies = [
        pltpu.make_async_copy(
            w_hbm.at[:, pl.ds(i * cw, cw)], w.at[i], loc_sem.at[CHUNKS + i]
        )
        for i in range(CHUNKS)
    ]
    g_copies = [
        pltpu.make_async_copy(g_hbm.at[:, pl.ds(i * cw, cw)], gath.at[z, i], loc_sem.at[i])
        for i in range(CHUNKS)
    ]
    for cp in g_copies:
        cp.start()
    for cp in w_copies:
        cp.start()

    down_pad[...] = jnp.zeros_like(down_pad)
    down_pad[:rank, :] = down_ref[...]
    mix_send[...] = dot(ao_ref[...], down_pad[...], NT).reshape(mix_send.shape)

    barrier = pltpu.get_barrier_semaphore()
    for k in range(1, ctx_n):
        pl.semaphore_signal(
            barrier, inc=1, device_id={"ctx": lax.rem(c + k, ctx_n), "tp": z}, device_id_type=MESH
        )
    for k in range(1, tp_n):
        pl.semaphore_signal(
            barrier, inc=1, device_id={"ctx": c, "tp": lax.rem(z + k, tp_n)}, device_id_type=MESH
        )
    pl.semaphore_wait(barrier, ctx_n - 1 + tp_n - 1)

    def ctx_copy(k, src, dst, s, r):
        return pltpu.make_async_remote_copy(
            src_ref=src, dst_ref=dst, send_sem=s.at[k], recv_sem=r.at[k],
            device_id={"ctx": lax.rem(c + k, ctx_n), "tp": z}, device_id_type=MESH,
        )

    def tp_copy(k, src, dst, s, r):
        return pltpu.make_async_remote_copy(
            src_ref=src, dst_ref=dst, send_sem=s.at[k], recv_sem=r.at[k],
            device_id={"ctx": c, "tp": lax.rem(z + k, tp_n)}, device_id_type=MESH,
        )

    def right_copy(s, i):
        return pltpu.make_async_remote_copy(
            src_ref=gath.at[z - s, i], dst_ref=gath.at[z - s, i],
            send_sem=gr_s.at[s, i], recv_sem=gr_r.at[s, i],
            device_id={"ctx": c, "tp": z + 1}, device_id_type=MESH,
        )

    def left_copy(s, i):
        return pltpu.make_async_remote_copy(
            src_ref=gath.at[z + s, i], dst_ref=gath.at[z + s, i],
            send_sem=gl_s.at[s, i], recv_sem=gl_r.at[s, i],
            device_id={"ctx": c, "tp": z - 1}, device_id_type=MESH,
        )

    def sends_right(s, i):
        last = tp_n - 1 if i >= kept else tp_n
        return jnp.logical_and(z - s >= 0, z + 1 < last)

    def sends_left(s, i):
        first = 1 if i >= kept else 0
        return jnp.logical_and(z + s < tp_n, z - 1 >= first)

    mix_copies = [
        tp_copy(k, mix_send.at[lax.rem(z + k, tp_n)], mix_recv.at[z], mix_s, mix_r)
        for k in range(1, tp_n)
    ]
    for cp in mix_copies:
        cp.start()
    mix_recv[z] = mix_send[z]

    moved = moved_chunks(tp_n)
    kept = CHUNKS - moved
    proj = w_hbm.shape[0]
    wr = proj // ctx_n
    is_edge = jnp.logical_or(z == 0, z == tp_n - 1)
    is_helper = jnp.logical_or(z == 1, z == tp_n - 2)
    inward = jnp.where(z == 0, 1, -1)
    beyond = jnp.where(z == 1, 1, -1)

    def wx_rows(j):
        return wx.at[:, pl.ds(pl.multiple_of(j * wr, wr), wr), :]

    edge_copy = None
    if moved:
        edge_copy = pltpu.make_async_remote_copy(
            src_ref=w.at[pl.ds(kept, moved), pl.ds(pl.multiple_of(c * wr, wr), wr), :],
            dst_ref=wx_rows(c), send_sem=we_s, recv_sem=we_r,
            device_id={"ctx": c, "tp": z + inward}, device_id_type=MESH,
        )

    for i in range(CHUNKS):
        g_copies[i].wait()

        @pl.when(sends_right(0, i))
        def _(i=i):
            right_copy(0, i).start()

        @pl.when(sends_left(0, i))
        def _(i=i):
            left_copy(0, i).start()

    for cp in w_copies:
        cp.wait()
    if moved:
        @pl.when(is_edge)
        def _():
            edge_copy.start()

    kv[c, 0] = k_ref[...]
    kv[c, 1] = v_ref[...]
    kv_copies = [ctx_copy(k, kv.at[c], kv.at[c], kv_s, kv_r) for k in range(1, ctx_n)]
    for cp in kv_copies:
        cp.start()

    cot_own = jnp.zeros((blk, rank), F32)
    for i in range(CHUNKS):
        cot_own += dot(gath[z, i], up_ref[:, i * cw : (i + 1) * cw], NT)
    cot[z] = jnp.zeros((blk, cot.shape[2]), BF16)
    cot[z, :, :rank] = cot_own.astype(BF16)
    cot_copies = [tp_copy(k, cot.at[z], cot.at[z], cot_s, cot_r) for k in range(1, tp_n)]
    for cp in cot_copies:
        cp.start()

    for part in range(2):
        for h in range(heads):
            q_st[part, h * half : (h + 1) * half, :] = q_ref[
                part * half : (part + 1) * half, h * hd : (h + 1) * hd
            ]
            ln_st[part, :, h * half : (h + 1) * half] = ln_ref[
                h : h + 1, part * half : (part + 1) * half
            ]
    dq_st[...] = jnp.zeros_like(dq_st)
    dkv_acc[...] = jnp.zeros_like(dkv_acc)

    def project(b, i):
        dacc[b] += dot(gath[b, i], w[i], NT)

    dacc[...] = jnp.zeros_like(dacc)
    for i in range(CHUNKS):
        project(z, i)

    def place(pair):
        early = pair <= c
        cell = jnp.where(early, pair, pair - c - 1)
        part = jnp.where(early, 0, 1)
        late_cell = cell >= ctx_n
        dev = jnp.where(late_cell, cells - 1 - cell, cell)
        start = pl.multiple_of(jnp.where(late_cell, half, 0), half)
        return early, cell, part, dev, start

    ctx_up_copies = [
        ctx_copy(k, u_send.at[lax.rem(c + k, ctx_n)], u_recv.at[c], u_s, u_r)
        for k in range(1, ctx_n)
    ]
    d_copies = [ctx_copy(k, d_recv.at[c], d_recv.at[c], d_s, d_r) for k in range(1, ctx_n)]
    rq = uz.shape[1]
    scattered = rq < rank

    def u_rows(t):
        return u_sum.at[pl.ds(pl.multiple_of(t * rq, rq), rq), :] if scattered else u_sum

    uz_copies = [
        tp_copy(k, u_rows(lax.rem(z + k, tp_n)), uz.at[z], uz_s, uz_r) for k in range(1, tp_n)
    ]
    uc_copies = []
    if scattered:
        uc_copies = [tp_copy(k, uc.at[z], uc.at[z], uc_s, uc_r) for k in range(1, tp_n)]
    ua_copies = [ctx_copy(k, u_all.at[c], u_all.at[c], ua_s, ua_r) for k in range(1, ctx_n)]

    def first_parts():
        for cp in mix_copies:
            cp.wait_recv()
        mixed = mix_recv[0]
        for t in range(1, tp_n):
            mixed += mix_recv[t]
        mixed = mixed.astype(BF16)
        for j in range(ctx_n):
            i, off = (j * uw) // cw, (j * uw) % cw
            part = dot(mixed, gath[z, i, :, off : off + uw], TN)
            u_send[j] = (adapter_scale_factor * part[:rank]).astype(BF16)
        for cp in ctx_up_copies:
            cp.start()
        u_recv[c] = u_send[c]

    def down_parts():
        for cp in cot_copies:
            cp.wait_recv()
        cot_rows = cot[...].reshape(rows, cot.shape[2])
        part = dot(cot_rows, ao_ref[...], TN)
        d_recv[c] = (adapter_scale_factor * part[:rank]).astype(BF16)
        for cp in d_copies:
            cp.start()

    def probabilities():
        for cp in kv_copies:
            cp.wait_recv()

        def body(pair, _):
            early, cell, part, dev, start = place(pair)
            keys = kv[dev, 0, pl.ds(start, half), :]
            scores = dot(keys, q_st[part], NT) * scale
            q_cell = jnp.where(early, c, cells - 1 - c)
            shape = (half, half)
            key_pos = cell * half + lax.broadcasted_iota(jnp.int32, shape, 0)
            q_pos = q_cell * half + lax.broadcasted_iota(jnp.int32, shape, 1)
            seen = q_pos >= key_pos
            for h in range(heads):
                cols = slice(h * half, (h + 1) * half)
                p = jnp.exp(scores[:, cols] - ln_st[part, :, cols])
                probs[pair, :, cols] = jnp.where(seen, p, 0.0)
            return 0

        lax.fori_loop(0, cells + 1, body, 0)

    def second_parts():
        for cp in ctx_up_copies:
            cp.wait_recv()
        total = u_recv[0].astype(F32)
        for j in range(1, ctx_n):
            total += u_recv[j].astype(F32)
        u_sum[...] = total.astype(BF16)
        for cp in uz_copies:
            cp.start()
        uz[z] = u_rows(z)[...]
        for cp in d_copies:
            cp.wait_recv()
        total = d_recv[0].astype(F32)
        for j in range(1, ctx_n):
            total += d_recv[j].astype(F32)
        down_out[...] = total

    def third_parts():
        for cp in uz_copies:
            cp.wait_recv()
        total = uz[0].astype(F32)
        for t in range(1, tp_n):
            total += uz[t].astype(F32)
        if scattered:
            uc[z] = total.astype(BF16)
            for cp in uc_copies:
                cp.start()
        else:
            u_all[c] = total.astype(BF16)

    def fourth_parts():
        if scattered:
            for cp in uc_copies:
                cp.wait_recv()
            u_all[c] = uc[...].reshape(u_all.shape[1:])
        for cp in ua_copies:
            cp.start()

    sibling = c + 1 - 2 * lax.rem(c, 2)
    own_rows = wx_rows(c) if moved else None
    wa_copies, wf_copies = [], []
    if moved:
        wa_copies = [
            ctx_copy(2 * k, own_rows, own_rows, wa_s, wa_r) for k in range(1, ctx_n // 2)
        ]
        for k in range(ctx_n // 2):
            block = wx_rows(lax.rem(c + ctx_n - 2 * k, ctx_n))
            wf_copies.append(
                pltpu.make_async_remote_copy(
                    src_ref=block, dst_ref=block, send_sem=wf_s.at[k], recv_sem=wf_r.at[k],
                    device_id={"ctx": sibling, "tp": z}, device_id_type=MESH,
                )
            )

    def px_copy(d):
        return pltpu.make_async_remote_copy(
            src_ref=px_send.at[d], dst_ref=px_recv.at[d], send_sem=px_s.at[d],
            recv_sem=px_r.at[d], device_id={"ctx": c, "tp": z - beyond}, device_id_type=MESH,
        )

    def weight_in():
        if moved:
            @pl.when(is_helper)
            def _():
                edge_copy.wait_recv()
                for cp in wa_copies:
                    cp.start()
                wf_copies[0].start()

    def weight_on():
        if moved:
            @pl.when(is_helper)
            def _():
                for k in range(1, ctx_n // 2):
                    wa_copies[k - 1].wait_recv()
                    wf_copies[k].start()

    def weight_whole():
        if moved:
            @pl.when(is_helper)
            def _():
                for cp in wf_copies:
                    cp.wait_recv()

    def help_with(d):
        if moved and d <= tp_n - 2:
            @pl.when(is_helper)
            def _():
                b = z + d * beyond
                part = dot(gath[b, kept], wx[0], NT)
                for i in range(1, moved):
                    part += dot(gath[b, kept + i], wx[i], NT)
                px_send[d] = part.astype(BF16)
                px_copy(d).start()

    for s in range(tp_n - 1):
        from_left = z - 1 - s >= 0
        from_right = z + 1 + s < tp_n
        for i in range(CHUNKS):
            @pl.when(jnp.logical_and(from_left, z < (tp_n - 1 if i >= kept else tp_n)))
            def _(s=s, i=i):
                right_copy(s, i).wait_recv()

                @pl.when(z + 1 < (tp_n - 1 if i >= kept else tp_n))
                def _():
                    pltpu.make_async_remote_copy(
                        src_ref=gath.at[z - 1 - s, i], dst_ref=gath.at[z - 1 - s, i],
                        send_sem=gr_s.at[s + 1, i], recv_sem=gr_r.at[s + 1, i],
                        device_id={"ctx": c, "tp": z + 1}, device_id_type=MESH,
                    ).start()

                project(z - 1 - s, i)

            @pl.when(jnp.logical_and(from_right, z > (0 if i >= kept else -1)))
            def _(s=s, i=i):
                left_copy(s, i).wait_recv()

                @pl.when(z - 1 >= (1 if i >= kept else 0))
                def _():
                    pltpu.make_async_remote_copy(
                        src_ref=gath.at[z + 1 + s, i], dst_ref=gath.at[z + 1 + s, i],
                        send_sem=gl_s.at[s + 1, i], recv_sem=gl_r.at[s + 1, i],
                        device_id={"ctx": c, "tp": z - 1}, device_id_type=MESH,
                    ).start()

                project(z + 1 + s, i)

            if s == 0 and i == 1:
                first_parts()
            if s == 0 and i == 4:
                down_parts()
            if s == 1 and i == 0:
                probabilities()
            if s == 1 and i == 2:
                weight_in()
            if s == 1 and i == 4:
                second_parts()
            if s == 1 and i == 6:
                third_parts()
            if s == 1 and i == CHUNKS - 1:
                weight_on()
                weight_whole()
                for d in range(min(3, tp_n - 1)):
                    help_with(d)
            if s >= 2 and i == CHUNKS - 1:
                help_with(s + 1)
            if s == 2 and i == 2:
                fourth_parts()

    if moved:
        @pl.when(is_edge)
        def _():
            for d in range(tp_n - 1):
                b = z + (d + 1) * inward
                pltpu.make_async_remote_copy(
                    src_ref=px_send.at[d], dst_ref=px_recv.at[d], send_sem=px_s.at[d],
                    recv_sem=px_r.at[d], device_id={"ctx": c, "tp": z + inward},
                    device_id_type=MESH,
                ).wait_recv()
                dacc[b] += px_recv[d].astype(F32)

    cot_rows = cot[...].reshape(rows, cot.shape[2])
    d_attn = dacc[...].reshape(rows, dacc.shape[2]) + adapter_scale_factor * dot(
        cot_rows, down_pad[...]
    )
    d_attn = d_attn.astype(BF16)
    for part in range(2):
        for h in range(heads):
            r0, c0 = part * half, h * hd
            block = d_attn[r0 : r0 + half, c0 : c0 + hd]
            do_st[part, h * half : (h + 1) * half, :] = block
            prod = block.astype(F32) * ao_ref[r0 : r0 + half, c0 : c0 + hd].astype(F32)
            delta_st[part, :, h * half : (h + 1) * half] = jnp.sum(prod.T, axis=0, keepdims=True)

    def backward(pair, _):
        early, cell, part, dev, start = place(pair)
        keys = kv[dev, 0, pl.ds(start, half), :]
        values = kv[dev, 1, pl.ds(start, half), :]
        p = probs[pair]
        grads = do_st[part]
        prob_grad = dot(values, grads, NT)
        score_grad = (p * (prob_grad - delta_st[part])).astype(BF16)
        dkv_acc[dev, 1, pl.ds(start, half), :] += dot(p.astype(BF16), grads)
        dkv_acc[dev, 0, pl.ds(start, half), :] += dot(score_grad, q_st[part])
        dq_st[part] += dot(score_grad, keys, TN)
        return 0

    lax.fori_loop(0, cells + 1, backward, 0)

    dkv_copies = [
        ctx_copy(k, dkv_send.at[lax.rem(c + k, ctx_n)], dkv_recv.at[c], dkv_s, dkv_r)
        for k in range(1, ctx_n)
    ]
    for k in list(range(1, ctx_n)):
        j = lax.rem(c + k, ctx_n)
        dkv_send[j, 0] = (dkv_acc[j, 0] * scale).astype(BF16)
        dkv_send[j, 1] = dkv_acc[j, 1].astype(BF16)
        dkv_copies[k - 1].start()
    dkv_recv[c, 0] = (dkv_acc[c, 0] * scale).astype(BF16)
    dkv_recv[c, 1] = dkv_acc[c, 1].astype(BF16)

    for part in range(2):
        for h in range(heads):
            dq_out[part * half : (part + 1) * half, h * hd : (h + 1) * hd] = (
                dq_st[part, h * half : (h + 1) * half, :] * scale
            ).astype(BF16)
    for cp in ua_copies:
        cp.wait_recv()
    for j in range(ctx_n):
        up_out[:, j * uw : (j + 1) * uw] = u_all[j]

    for cp in dkv_copies:
        cp.wait_recv()
    total = dkv_recv[0].astype(F32)
    for j in range(1, ctx_n):
        total += dkv_recv[j].astype(F32)
    pair_buf[0] = total.astype(BF16)
    other = z + 1 - 2 * lax.rem(z, 2)
    pair_copy = pltpu.make_async_remote_copy(
        src_ref=pair_buf.at[0], dst_ref=pair_buf.at[1], send_sem=pair_s, recv_sem=pair_r,
        device_id={"ctx": c, "tp": other}, device_id_type=MESH,
    )
    pair_copy.start()
    pair_copy.wait_recv()
    sums = pair_buf[0].astype(F32) + pair_buf[1].astype(F32)
    dk_out[...] = sums[0].astype(BF16)
    dv_out[...] = sums[1].astype(BF16)

    for group in (
        kv_copies, cot_copies, mix_copies, ctx_up_copies, d_copies, uz_copies, uc_copies,
        ua_copies, dkv_copies,
    ):
        for cp in group:
            cp.wait_send()
    pair_copy.wait_send()
    if moved:
        @pl.when(is_edge)
        def _():
            edge_copy.wait_send()

        @pl.when(is_helper)
        def _():
            for cp in wa_copies + wf_copies:
                cp.wait_send()
            for d in range(tp_n - 1):
                px_copy(d).wait_send()
    for s in range(tp_n - 1):
        for i in range(CHUNKS):
            @pl.when(sends_right(s, i))
            def _(s=s, i=i):
                right_copy(s, i).wait_send()

            @pl.when(sends_left(s, i))
            def _(s=s, i=i):
                left_copy(s, i).wait_send()


def moved_chunks(tp_n):
    return MOVED if tp_n == 4 else 0


def hand_on(*refs):
    n = len(refs) // 2
    for i in range(n):
        refs[n + i][...] = refs[i][...]


def handed_on(*arrays):
    vmem = pl.BlockSpec(memory_space=pltpu.VMEM)
    return pl.pallas_call(
        hand_on,
        out_shape=tuple(jax.ShapeDtypeStruct(a.shape, a.dtype) for a in arrays),
        in_specs=[vmem] * len(arrays),
        out_specs=(vmem,) * len(arrays),
    )(*arrays)


def local(q, k, v, ao, ln, g, w, down, up):
    ctx_n = lax.axis_size("ctx")
    tp_n = lax.axis_size("tp")
    rows, q_cols = q.shape
    heads = ln.shape[0]
    hd = q_cols // heads
    half = rows // 2
    blk = rows // tp_n
    width = g.shape[1]
    cw = width // CHUNKS
    uw = width // ctx_n
    proj = w.shape[0]
    rank = down.shape[1]
    moves = moved_chunks(tp_n) > 0
    rq = rank // tp_n if rank % (16 * tp_n) == 0 else rank
    lanes = max(128, rank)
    pairs = 2 * ctx_n + 1
    vmem = pl.BlockSpec(memory_space=pltpu.VMEM)
    hbm = pl.BlockSpec(memory_space=pl.ANY)
    V = pltpu.VMEM
    DMA = pltpu.SemaphoreType.DMA
    scratch = [
        V((tp_n, CHUNKS, blk, cw), BF16),
        V((CHUNKS, proj, cw), BF16),
        V((tp_n, blk, proj), F32),
        V((lanes, proj), BF16),
        V((tp_n, blk, lanes), BF16),
        V((tp_n, blk, lanes), F32),
        V((tp_n, blk, lanes), F32),
        V((ctx_n, rank, uw), BF16),
        V((ctx_n, rank, uw), BF16),
        V((rank, uw), BF16),
        V((tp_n, rq, uw), BF16),
        V((tp_n, rq, uw), BF16),
        V((ctx_n, rank, uw), BF16),
        V((MOVED, proj, cw) if moves else (1, 16, 128), BF16),
        V((tp_n, blk, proj) if moves else (1, 16, 128), BF16),
        V((tp_n, blk, proj) if moves else (1, 16, 128), BF16),
        V((ctx_n, rank, proj), BF16),
        V((ctx_n, 2, rows, hd), BF16),
        V((pairs, half, heads * half), F32),
        V((2, heads * half, hd), BF16),
        V((2, heads * half, hd), BF16),
        V((2, 1, heads * half), F32),
        V((2, 1, heads * half), F32),
        V((2, heads * half, hd), F32),
        V((ctx_n, 2, rows, hd), F32),
        V((ctx_n, 2, rows, hd), BF16),
        V((ctx_n, 2, rows, hd), BF16),
        V((2, 2, rows, hd), BF16),
        DMA((2 * CHUNKS,)),
    ]
    scratch += [DMA((tp_n, CHUNKS))] * 4
    scratch += [DMA((ctx_n,))] * 2 + [DMA((tp_n,))] * 4 + [DMA((ctx_n,))] * 2
    scratch += [DMA((tp_n,))] * 4 + [DMA((ctx_n,))] * 6 + [DMA((tp_n,))] * 2
    scratch += [DMA((ctx_n,))] * 4 + [DMA] * 4
    dq, dk, dv, dd, du = pl.pallas_call(
        functools.partial(kernel, ctx_n, tp_n, heads),
        out_shape=(
            jax.ShapeDtypeStruct(q.shape, BF16),
            jax.ShapeDtypeStruct(k.shape, BF16),
            jax.ShapeDtypeStruct(v.shape, BF16),
            jax.ShapeDtypeStruct((rank, proj), F32),
            jax.ShapeDtypeStruct(up.shape, BF16),
        ),
        in_specs=[vmem] * 5 + [hbm] * 2 + [vmem] * 2,
        out_specs=(vmem,) * 5,
        scratch_shapes=scratch,
        compiler_params=pltpu.CompilerParams(
            collective_id=0, has_side_effects=True, vmem_limit_bytes=60 * 2**20
        ),
        cost_estimate=pl.CostEstimate(
            flops=5 * 10**9, bytes_accessed=16 * 2**20, transcendentals=2**21
        ),
    )(q, k, v, ao, ln, g, w, down.T, up)
    dq, dk, dv, dd, du = handed_on(dq, dk, dv, dd, du)
    return dq, dk, dv, dd.T, du


def solution(mesh):
    placed = (
        P("ctx", "tp"),
        P("ctx", "tp"),
        P("ctx", "tp"),
        P("ctx", "tp"),
        P("tp", "ctx"),
        P(("ctx", "tp"), None),
        P("tp", None),
        P("tp", None),
        P(),
    )
    return jax.shard_map(
        local,
        mesh=mesh,
        in_specs=placed,
        out_specs=(P("ctx", "tp"), P("ctx", "tp"), P("ctx", "tp"), P("tp", None), P()),
        check_vma=False,
    )
```

```python
import functools

import jax
import jax.numpy as jnp
from jax import lax
from jax.experimental import pallas as pl
from jax.experimental.pallas import tpu as pltpu
from jax.sharding import PartitionSpec as P

adapter_scale_factor = 2.0
MESH = pl.DeviceIdType.MESH
F32 = jnp.float32
BF16 = jnp.bfloat16
NT = (((1,), (1,)), ((), ()))
TN = (((0,), (0,)), ((), ()))
CHUNKS = 8
AHEAD = 3
MOVED = 3
KEPT = CHUNKS - MOVED


def dot(a, b, dims=(((1,), (0,)), ((), ()))):
    return lax.dot_general(a, b, dims, preferred_element_type=F32)


def kernel(
    ctx_n, tp_n, heads,
    q_ref, k_ref, v_ref, ao_ref, ln_ref, g_hbm, w_hbm, down_ref, up_ref,
    dq_out, dk_out, dv_out, down_out, up_out,
    gath, w, dacc, down_pad,
    cot, mix_send, mix_recv,
    u_send, u_recv, u_sum, uz, uc, u_all, wx, px_send, px_recv,
    d_recv, kv, probs, q_st, do_st, ln_st, delta_st, dq_st,
    dkv_acc, dkv_send, dkv_recv, pair_buf,
    loc_sem, gr_s, gr_r, gl_s, gl_r,
    kv_s, kv_r, cot_s, cot_r, mix_s, mix_r, u_s, u_r, uz_s, uz_r, uc_s, uc_r, ua_s, ua_r,
    d_s, d_r, dkv_s, dkv_r, px_s, px_r, wa_s, wa_r, half_s, half_r, we_s, we_r, pair_s, pair_r,
):
    c = lax.axis_index("ctx")
    z = lax.axis_index("tp")
    rows = q_ref.shape[0]
    half = rows // 2
    blk = rows // tp_n
    width = g_hbm.shape[1]
    cw = width // CHUNKS
    uw = width // ctx_n
    rank = down_ref.shape[0]
    hd = q_ref.shape[1] // heads
    scale = hd ** (-0.5)
    cells = 2 * ctx_n

    w_copies = [
        pltpu.make_async_copy(
            w_hbm.at[:, pl.ds(i * cw, cw)], w.at[i], loc_sem.at[CHUNKS + i]
        )
        for i in range(CHUNKS)
    ]
    g_copies = [
        pltpu.make_async_copy(g_hbm.at[:, pl.ds(i * cw, cw)], gath.at[z, i], loc_sem.at[i])
        for i in range(CHUNKS)
    ]
    for cp in g_copies:
        cp.start()
    for cp in w_copies:
        cp.start()

    down_pad[...] = jnp.zeros_like(down_pad)
    down_pad[:rank, :] = down_ref[...]
    mix_send[...] = dot(ao_ref[...], down_pad[...], NT).reshape(mix_send.shape)

    barrier = pltpu.get_barrier_semaphore()
    for k in range(1, ctx_n):
        pl.semaphore_signal(
            barrier, inc=1, device_id={"ctx": lax.rem(c + k, ctx_n), "tp": z}, device_id_type=MESH
        )
    for k in range(1, tp_n):
        pl.semaphore_signal(
            barrier, inc=1, device_id={"ctx": c, "tp": lax.rem(z + k, tp_n)}, device_id_type=MESH
        )
    pl.semaphore_wait(barrier, ctx_n - 1 + tp_n - 1)

    def ctx_copy(k, src, dst, s, r):
        return pltpu.make_async_remote_copy(
            src_ref=src, dst_ref=dst, send_sem=s.at[k], recv_sem=r.at[k],
            device_id={"ctx": lax.rem(c + k, ctx_n), "tp": z}, device_id_type=MESH,
        )

    def tp_copy(k, src, dst, s, r):
        return pltpu.make_async_remote_copy(
            src_ref=src, dst_ref=dst, send_sem=s.at[k], recv_sem=r.at[k],
            device_id={"ctx": c, "tp": lax.rem(z + k, tp_n)}, device_id_type=MESH,
        )

    def right_copy(s, i):
        return pltpu.make_async_remote_copy(
            src_ref=gath.at[z - s, i], dst_ref=gath.at[z - s, i],
            send_sem=gr_s.at[s, i], recv_sem=gr_r.at[s, i],
            device_id={"ctx": c, "tp": z + 1}, device_id_type=MESH,
        )

    def left_copy(s, i):
        return pltpu.make_async_remote_copy(
            src_ref=gath.at[z + s, i], dst_ref=gath.at[z + s, i],
            send_sem=gl_s.at[s, i], recv_sem=gl_r.at[s, i],
            device_id={"ctx": c, "tp": z - 1}, device_id_type=MESH,
        )

    def sends_right(s, i):
        last = tp_n - 1 if i >= kept else tp_n
        return jnp.logical_and(z - s >= 0, z + 1 < last)

    def sends_left(s, i):
        first = 1 if i >= kept else 0
        return jnp.logical_and(z + s < tp_n, z - 1 >= first)

    mix_copies = [
        tp_copy(k, mix_send.at[lax.rem(z + k, tp_n)], mix_recv.at[z], mix_s, mix_r)
        for k in range(1, tp_n)
    ]
    for cp in mix_copies:
        cp.start()
    mix_recv[z] = mix_send[z]

    moved = moved_chunks(tp_n)
    kept = CHUNKS - moved
    proj = w_hbm.shape[0]
    wr = proj // ctx_n
    is_edge = jnp.logical_or(z == 0, z == tp_n - 1)
    is_helper = jnp.logical_or(z == 1, z == tp_n - 2)
    inward = jnp.where(z == 0, 1, -1)
    beyond = jnp.where(z == 1, 1, -1)

    def wx_rows(j):
        return wx.at[:, pl.ds(pl.multiple_of(j * wr, wr), wr), :]

    edge_copy = None
    if moved:
        edge_copy = pltpu.make_async_remote_copy(
            src_ref=w.at[pl.ds(kept, moved), pl.ds(pl.multiple_of(c * wr, wr), wr), :],
            dst_ref=wx_rows(c), send_sem=we_s, recv_sem=we_r,
            device_id={"ctx": c, "tp": z + inward}, device_id_type=MESH,
        )

    def out_right(t, more=True):
        s, i = divmod(t, CHUNKS)
        if s < tp_n - 1:
            @pl.when(jnp.logical_and(sends_right(s, i), more))
            def _():
                right_copy(s, i).start()

    def out_left(t, more=True):
        s, i = divmod(t, CHUNKS)
        if s < tp_n - 1:
            @pl.when(jnp.logical_and(sends_left(s, i), more))
            def _():
                left_copy(s, i).start()

    for i in range(CHUNKS):
        g_copies[i].wait()
        if i < AHEAD:
            out_right(i)
            out_left(i)

    for cp in w_copies:
        cp.wait()
    sibling = c + 1 - 2 * lax.rem(c, 2)
    chips = ctx_n // 2

    def sibling_copy(src, dst, s, r):
        return pltpu.make_async_remote_copy(
            src_ref=src, dst_ref=dst, send_sem=s, recv_sem=r,
            device_id={"ctx": sibling, "tp": z}, device_id_type=MESH,
        )

    def shared_gather(at, s, r):
        out = [ctx_copy(2 * k, at(c), at(c), s, r) for k in range(1, chips)]
        on = []
        for k in range(chips):
            block = at(lax.rem(c + ctx_n - 2 * k, ctx_n))
            on.append(sibling_copy(block, block, s.at[2 * k + 1], r.at[2 * k + 1]))
        return out, on

    def hand_over(out, on):
        for k in range(1, chips):
            out[k - 1].wait_recv()
            on[k].start()

    kv[c, 0] = k_ref[...]
    kv[c, 1] = v_ref[...]
    kv_out, kv_on = shared_gather(lambda j: kv.at[j], kv_s, kv_r)
    for cp in kv_out + kv_on[:1]:
        cp.start()

    cot_own = jnp.zeros((blk, rank), F32)
    for i in range(CHUNKS):
        cot_own += dot(gath[z, i], up_ref[:, i * cw : (i + 1) * cw], NT)
    cot[z] = jnp.zeros((blk, cot.shape[2]), BF16)
    cot[z, :, :rank] = cot_own.astype(BF16)
    cot_copies = [tp_copy(k, cot.at[z], cot.at[z], cot_s, cot_r) for k in range(1, tp_n)]
    for cp in cot_copies:
        cp.start()

    for part in range(2):
        for h in range(heads):
            q_st[part, h * half : (h + 1) * half, :] = q_ref[
                part * half : (part + 1) * half, h * hd : (h + 1) * hd
            ]
            ln_st[part, :, h * half : (h + 1) * half] = ln_ref[
                h : h + 1, part * half : (part + 1) * half
            ]
    dq_st[...] = jnp.zeros_like(dq_st)
    dkv_acc[...] = jnp.zeros_like(dkv_acc)

    def project(b, i):
        dacc[b] += dot(gath[b, i], w[i], NT)

    dacc[...] = jnp.zeros_like(dacc)

    def place(pair):
        early = pair <= c
        cell = jnp.where(early, pair, pair - c - 1)
        part = jnp.where(early, 0, 1)
        late_cell = cell >= ctx_n
        dev = jnp.where(late_cell, cells - 1 - cell, cell)
        start = pl.multiple_of(jnp.where(late_cell, half, 0), half)
        return early, cell, part, dev, start

    ctx_up_copies = [
        ctx_copy(k, u_send.at[lax.rem(c + k, ctx_n)], u_recv.at[c], u_s, u_r)
        for k in range(1, ctx_n)
    ]
    d_copies = [ctx_copy(k, d_recv.at[c], d_recv.at[c], d_s, d_r) for k in range(1, ctx_n)]
    rq = uz.shape[1]
    scattered = rq < rank

    def u_rows(t):
        return u_sum.at[pl.ds(pl.multiple_of(t * rq, rq), rq), :] if scattered else u_sum

    uz_copies = [
        tp_copy(k, u_rows(lax.rem(z + k, tp_n)), uz.at[z], uz_s, uz_r) for k in range(1, tp_n)
    ]
    uc_copies = []
    if scattered:
        uc_copies = [tp_copy(k, uc.at[z], uc.at[z], uc_s, uc_r) for k in range(1, tp_n)]
    ua_out, ua_on = shared_gather(lambda j: u_all.at[j], ua_s, ua_r)

    def first_parts():
        for cp in mix_copies:
            cp.wait_recv()
        mixed = mix_recv[0]
        for t in range(1, tp_n):
            mixed += mix_recv[t]
        mixed = mixed.astype(BF16)
        for j in range(ctx_n):
            i, off = (j * uw) // cw, (j * uw) % cw
            part = dot(mixed, gath[z, i, :, off : off + uw], TN)
            u_send[j] = (adapter_scale_factor * part[:rank]).astype(BF16)
        for cp in ctx_up_copies:
            cp.start()
        u_recv[c] = u_send[c]

    def down_parts():
        for cp in cot_copies:
            cp.wait_recv()
        cot_rows = cot[...].reshape(rows, cot.shape[2])
        part = dot(cot_rows, ao_ref[...], TN)
        d_recv[c] = (adapter_scale_factor * part[:rank]).astype(BF16)
        for cp in d_copies:
            cp.start()

    def probabilities():
        for cp in kv_on:
            cp.wait_recv()

        def body(pair, _):
            early, cell, part, dev, start = place(pair)
            keys = kv[dev, 0, pl.ds(start, half), :]
            scores = dot(keys, q_st[part], NT) * scale
            q_cell = jnp.where(early, c, cells - 1 - c)
            shape = (half, half)
            key_pos = cell * half + lax.broadcasted_iota(jnp.int32, shape, 0)
            q_pos = q_cell * half + lax.broadcasted_iota(jnp.int32, shape, 1)
            seen = q_pos >= key_pos
            for h in range(heads):
                cols = slice(h * half, (h + 1) * half)
                p = jnp.exp(scores[:, cols] - ln_st[part, :, cols])
                probs[pair, :, cols] = jnp.where(seen, p, 0.0)
            return 0

        lax.fori_loop(0, cells + 1, body, 0)

    def second_parts():
        for cp in ctx_up_copies:
            cp.wait_recv()
        total = u_recv[0].astype(F32)
        for j in range(1, ctx_n):
            total += u_recv[j].astype(F32)
        u_sum[...] = total.astype(BF16)
        for cp in uz_copies:
            cp.start()
        uz[z] = u_rows(z)[...]
        for cp in d_copies:
            cp.wait_recv()
        total = d_recv[0].astype(F32)
        for j in range(1, ctx_n):
            total += d_recv[j].astype(F32)
        down_out[...] = total

    def third_parts():
        for cp in uz_copies:
            cp.wait_recv()
        total = uz[0].astype(F32)
        for t in range(1, tp_n):
            total += uz[t].astype(F32)
        if scattered:
            uc[z] = total.astype(BF16)
            for cp in uc_copies:
                cp.start()
        else:
            u_all[c] = total.astype(BF16)

    def fourth_parts():
        if scattered:
            for cp in uc_copies:
                cp.wait_recv()
            u_all[c] = uc[...].reshape(u_all.shape[1:])
        for cp in ua_out + ua_on[:1]:
            cp.start()

    wa_copies, wf_copies = [], []
    if moved:
        wa_copies, wf_copies = shared_gather(wx_rows, wa_s, wa_r)

    def px_copy(d):
        return pltpu.make_async_remote_copy(
            src_ref=px_send.at[d], dst_ref=px_recv.at[d], send_sem=px_s.at[d],
            recv_sem=px_r.at[d], device_id={"ctx": c, "tp": z - beyond}, device_id_type=MESH,
        )

    def weight_in():
        if moved:
            @pl.when(is_helper)
            def _():
                edge_copy.wait_recv()
                for cp in wa_copies:
                    cp.start()
                wf_copies[0].start()

    def weight_on():
        if moved:
            @pl.when(is_helper)
            def _():
                hand_over(wa_copies, wf_copies)

    def weight_whole():
        if moved:
            @pl.when(is_helper)
            def _():
                for cp in wf_copies:
                    cp.wait_recv()

    def help_with(d):
        if moved and d <= tp_n - 2:
            @pl.when(is_helper)
            def _():
                b = z + d * beyond
                part = dot(gath[b, kept], wx[0], NT)
                for i in range(1, moved):
                    part += dot(gath[b, kept + i], wx[i], NT)
                px_send[d] = part.astype(BF16)
                px_copy(d).start()

    edge_right = jnp.logical_and(z + 1 == tp_n - 1, moved > 0)
    edge_left = jnp.logical_and(z - 1 == 0, moved > 0)
    for s in range(tp_n - 1):
        for i in range(CHUNKS):
            got_left = jnp.logical_and(z - 1 - s >= 0, z < (tp_n - 1 if i >= kept else tp_n))
            got_right = jnp.logical_and(z + 1 + s < tp_n, z > (0 if i >= kept else -1))

            @pl.when(got_left)
            def _(s=s, i=i):
                right_copy(s, i).wait_recv()

            @pl.when(got_right)
            def _(s=s, i=i):
                left_copy(s, i).wait_recv()

            t = s * CHUNKS + i
            first = t + AHEAD < CHUNKS
            out_right(t + AHEAD, first or jnp.logical_not(edge_right))
            out_left(t + AHEAD, first or jnp.logical_not(edge_left))
            out_right(t + CHUNKS, edge_right)
            out_left(t + CHUNKS, edge_left)
            if moved and t == CHUNKS - AHEAD:
                @pl.when(is_edge)
                def _():
                    edge_copy.start()
            if s == 0:
                project(z, i)

            @pl.when(got_left)
            def _(s=s, i=i):
                project(z - 1 - s, i)

            @pl.when(got_right)
            def _(s=s, i=i):
                project(z + 1 + s, i)

            if s == 0 and i == 1:
                first_parts()
            if s == 0 and i == 4:
                down_parts()
            if s == 0 and i == 6:
                hand_over(kv_out, kv_on)
            if s == 1 and i == 0:
                probabilities()
            if s == 1 and i == 2:
                weight_in()
            if s == 1 and i == 4:
                second_parts()
            if s == 1 and i == 6:
                third_parts()
            if s == 1 and i == CHUNKS - 1:
                weight_on()
                weight_whole()
                for d in range(min(3, tp_n - 1)):
                    help_with(d)
            if s >= 2 and i == CHUNKS - 1:
                help_with(s + 1)
            if s == 2 and i == 2:
                fourth_parts()

    if moved:
        @pl.when(is_edge)
        def _():
            for d in range(tp_n - 1):
                b = z + (d + 1) * inward
                pltpu.make_async_remote_copy(
                    src_ref=px_send.at[d], dst_ref=px_recv.at[d], send_sem=px_s.at[d],
                    recv_sem=px_r.at[d], device_id={"ctx": c, "tp": z + inward},
                    device_id_type=MESH,
                ).wait_recv()
                dacc[b] += px_recv[d].astype(F32)

    cot_rows = cot[...].reshape(rows, cot.shape[2])
    d_attn = dacc[...].reshape(rows, dacc.shape[2]) + adapter_scale_factor * dot(
        cot_rows, down_pad[...]
    )
    d_attn = d_attn.astype(BF16)
    for part in range(2):
        for h in range(heads):
            r0, c0 = part * half, h * hd
            block = d_attn[r0 : r0 + half, c0 : c0 + hd]
            do_st[part, h * half : (h + 1) * half, :] = block
            prod = block.astype(F32) * ao_ref[r0 : r0 + half, c0 : c0 + hd].astype(F32)
            delta_st[part, :, h * half : (h + 1) * half] = jnp.sum(prod.T, axis=0, keepdims=True)

    def backward(pair, _):
        early, cell, part, dev, start = place(pair)
        keys = kv[dev, 0, pl.ds(start, half), :]
        values = kv[dev, 1, pl.ds(start, half), :]
        p = probs[pair]
        grads = do_st[part]
        prob_grad = dot(values, grads, NT)
        score_grad = (p * (prob_grad - delta_st[part])).astype(BF16)
        dkv_acc[dev, 1, pl.ds(start, half), :] += dot(p.astype(BF16), grads)
        dkv_acc[dev, 0, pl.ds(start, half), :] += dot(score_grad, q_st[part])
        dq_st[part] += dot(score_grad, keys, TN)
        return 0

    lax.fori_loop(0, cells + 1, backward, 0)

    side = lax.rem(c, 2)
    chip = c // 2
    half_copy = sibling_copy(dkv_send.at[1 - side], dkv_recv.at[0], half_s, half_r)
    for m in range(chips):
        dkv_send[1 - side, m, 0] = (dkv_acc[2 * m + 1 - side, 0] * scale).astype(BF16)
        dkv_send[1 - side, m, 1] = dkv_acc[2 * m + 1 - side, 1].astype(BF16)
    half_copy.start()
    hand_over(ua_out, ua_on)
    half_copy.wait_recv()
    dkv_copies = []
    for k in list(range(1, chips)) + [0]:
        m = lax.rem(chip + k, chips)
        for n, factor in ((0, scale), (1, 1.0)):
            sums = dkv_acc[2 * m + side, n] * factor + dkv_recv[0, m, n].astype(F32)
            if k:
                dkv_send[side, m, n] = sums.astype(BF16)
            else:
                dkv_recv[1, m, n] = sums.astype(BF16)
        if k:
            dkv_copies.append(
                ctx_copy(2 * k, dkv_send.at[side, m], dkv_recv.at[1, chip], dkv_s, dkv_r)
            )
            dkv_copies[-1].start()

    for part in range(2):
        for h in range(heads):
            dq_out[part * half : (part + 1) * half, h * hd : (h + 1) * hd] = (
                dq_st[part, h * half : (h + 1) * half, :] * scale
            ).astype(BF16)
    for cp in ua_on:
        cp.wait_recv()
    for j in range(ctx_n):
        up_out[:, j * uw : (j + 1) * uw] = u_all[j]

    for cp in dkv_copies:
        cp.wait_recv()
    total = dkv_recv[1, 0].astype(F32)
    for m in range(1, chips):
        total += dkv_recv[1, m].astype(F32)
    pair_buf[0] = total.astype(BF16)
    other = z + 1 - 2 * lax.rem(z, 2)
    pair_copy = pltpu.make_async_remote_copy(
        src_ref=pair_buf.at[0], dst_ref=pair_buf.at[1], send_sem=pair_s, recv_sem=pair_r,
        device_id={"ctx": c, "tp": other}, device_id_type=MESH,
    )
    pair_copy.start()
    pair_copy.wait_recv()
    sums = pair_buf[0].astype(F32) + pair_buf[1].astype(F32)
    dk_out[...] = sums[0].astype(BF16)
    dv_out[...] = sums[1].astype(BF16)

    for group in (
        kv_out, kv_on, cot_copies, mix_copies, ctx_up_copies, d_copies, uz_copies, uc_copies,
        ua_out, ua_on, [half_copy], dkv_copies,
    ):
        for cp in group:
            cp.wait_send()
    pair_copy.wait_send()
    if moved:
        @pl.when(is_edge)
        def _():
            edge_copy.wait_send()

        @pl.when(is_helper)
        def _():
            for cp in wa_copies + wf_copies:
                cp.wait_send()
            for d in range(tp_n - 1):
                px_copy(d).wait_send()
    for s in range(tp_n - 1):
        for i in range(CHUNKS):
            @pl.when(sends_right(s, i))
            def _(s=s, i=i):
                right_copy(s, i).wait_send()

            @pl.when(sends_left(s, i))
            def _(s=s, i=i):
                left_copy(s, i).wait_send()


def moved_chunks(tp_n):
    return MOVED if tp_n == 4 else 0


def hand_on(*refs):
    n = len(refs) // 2
    for i in range(n):
        refs[n + i][...] = refs[i][...]


def handed_on(*arrays):
    vmem = pl.BlockSpec(memory_space=pltpu.VMEM)
    return pl.pallas_call(
        hand_on,
        out_shape=tuple(jax.ShapeDtypeStruct(a.shape, a.dtype) for a in arrays),
        in_specs=[vmem] * len(arrays),
        out_specs=(vmem,) * len(arrays),
    )(*arrays)


def local(q, k, v, ao, ln, g, w, down, up):
    ctx_n = lax.axis_size("ctx")
    tp_n = lax.axis_size("tp")
    rows, q_cols = q.shape
    heads = ln.shape[0]
    hd = q_cols // heads
    half = rows // 2
    blk = rows // tp_n
    width = g.shape[1]
    cw = width // CHUNKS
    uw = width // ctx_n
    proj = w.shape[0]
    rank = down.shape[1]
    moves = moved_chunks(tp_n) > 0
    rq = rank // tp_n if rank % (16 * tp_n) == 0 else rank
    lanes = max(128, rank)
    pairs = 2 * ctx_n + 1
    vmem = pl.BlockSpec(memory_space=pltpu.VMEM)
    hbm = pl.BlockSpec(memory_space=pl.ANY)
    V = pltpu.VMEM
    DMA = pltpu.SemaphoreType.DMA
    scratch = [
        V((tp_n, CHUNKS, blk, cw), BF16),
        V((CHUNKS, proj, cw), BF16),
        V((tp_n, blk, proj), F32),
        V((lanes, proj), BF16),
        V((tp_n, blk, lanes), BF16),
        V((tp_n, blk, lanes), F32),
        V((tp_n, blk, lanes), F32),
        V((ctx_n, rank, uw), BF16),
        V((ctx_n, rank, uw), BF16),
        V((rank, uw), BF16),
        V((tp_n, rq, uw), BF16),
        V((tp_n, rq, uw), BF16),
        V((ctx_n, rank, uw), BF16),
        V((MOVED, proj, cw) if moves else (1, 16, 128), BF16),
        V((tp_n, blk, proj) if moves else (1, 16, 128), BF16),
        V((tp_n, blk, proj) if moves else (1, 16, 128), BF16),
        V((ctx_n, rank, proj), BF16),
        V((ctx_n, 2, rows, hd), BF16),
        V((pairs, half, heads * half), F32),
        V((2, heads * half, hd), BF16),
        V((2, heads * half, hd), BF16),
        V((2, 1, heads * half), F32),
        V((2, 1, heads * half), F32),
        V((2, heads * half, hd), F32),
        V((ctx_n, 2, rows, hd), F32),
        V((2, ctx_n // 2, 2, rows, hd), BF16),
        V((2, ctx_n // 2, 2, rows, hd), BF16),
        V((2, 2, rows, hd), BF16),
        DMA((2 * CHUNKS,)),
    ]
    scratch += [DMA((tp_n, CHUNKS))] * 4
    scratch += [DMA((ctx_n,))] * 2 + [DMA((tp_n,))] * 4 + [DMA((ctx_n,))] * 2
    scratch += [DMA((tp_n,))] * 4 + [DMA((ctx_n,))] * 6 + [DMA((tp_n,))] * 2
    scratch += [DMA((ctx_n,))] * 2 + [DMA] * 6
    dq, dk, dv, dd, du = pl.pallas_call(
        functools.partial(kernel, ctx_n, tp_n, heads),
        out_shape=(
            jax.ShapeDtypeStruct(q.shape, BF16),
            jax.ShapeDtypeStruct(k.shape, BF16),
            jax.ShapeDtypeStruct(v.shape, BF16),
            jax.ShapeDtypeStruct((rank, proj), F32),
            jax.ShapeDtypeStruct(up.shape, BF16),
        ),
        in_specs=[vmem] * 5 + [hbm] * 2 + [vmem] * 2,
        out_specs=(vmem,) * 5,
        scratch_shapes=scratch,
        compiler_params=pltpu.CompilerParams(
            collective_id=0, has_side_effects=True, vmem_limit_bytes=60 * 2**20
        ),
        cost_estimate=pl.CostEstimate(
            flops=5 * 10**9, bytes_accessed=16 * 2**20, transcendentals=2**21
        ),
    )(q, k, v, ao, ln, g, w, down.T, up)
    dq, dk, dv, dd, du = handed_on(dq, dk, dv, dd, du)
    return dq, dk, dv, dd.T, du


def solution(mesh):
    placed = (
        P("ctx", "tp"),
        P("ctx", "tp"),
        P("ctx", "tp"),
        P("ctx", "tp"),
        P("tp", "ctx"),
        P(("ctx", "tp"), None),
        P("tp", None),
        P("tp", None),
        P(),
    )
    return jax.shard_map(
        local,
        mesh=mesh,
        in_specs=placed,
        out_specs=(P("ctx", "tp"), P("ctx", "tp"), P("ctx", "tp"), P("tp", None), P()),
        check_vma=False,
    )
```

```python
import functools

import jax
import jax.numpy as jnp
from jax import lax
from jax.experimental import pallas as pl
from jax.experimental.pallas import tpu as pltpu
from jax.sharding import PartitionSpec as P

adapter_scale_factor = 2.0
MESH = pl.DeviceIdType.MESH
F32 = jnp.float32
BF16 = jnp.bfloat16
NT = (((1,), (1,)), ((), ()))
TN = (((0,), (0,)), ((), ()))
CHUNKS = 8
AHEAD = 3
MOVED = 2
KEPT = CHUNKS - MOVED


def dot(a, b, dims=(((1,), (0,)), ((), ()))):
    return lax.dot_general(a, b, dims, preferred_element_type=F32)


def kernel(
    ctx_n, tp_n, heads,
    q_ref, k_ref, v_ref, ao_ref, ln_ref, g_hbm, w_hbm, down_ref, up_ref,
    dq_out, dk_out, dv_out, down_out, up_out,
    gath, w, dacc, down_pad,
    cot, mix_send, mix_recv,
    u_send, u_recv, u_sum, uz, uc, u_all, wx, px_send, px_recv,
    d_recv, kv, probs, q_st, do_st, ln_st, delta_st, dq_st,
    dkv_acc, dkv_send, dkv_recv, pair_buf,
    loc_sem, gr_s, gr_r, gl_s, gl_r,
    kv_s, kv_r, cot_s, cot_r, mix_s, mix_r, u_s, u_r, uz_s, uz_r, uc_s, uc_r, ua_s, ua_r,
    d_s, d_r, dkv_s, dkv_r, px_s, px_r, wa_s, wa_r, half_s, half_r, we_s, we_r, pair_s, pair_r,
):
    c = lax.axis_index("ctx")
    z = lax.axis_index("tp")
    rows = q_ref.shape[0]
    half = rows // 2
    blk = rows // tp_n
    width = g_hbm.shape[1]
    cw = width // CHUNKS
    uw = width // ctx_n
    rank = down_ref.shape[0]
    hd = q_ref.shape[1] // heads
    scale = hd ** (-0.5)
    cells = 2 * ctx_n

    w_copies = [
        pltpu.make_async_copy(
            w_hbm.at[:, pl.ds(i * cw, cw)], w.at[i], loc_sem.at[CHUNKS + i]
        )
        for i in range(CHUNKS)
    ]
    g_copies = [
        pltpu.make_async_copy(g_hbm.at[:, pl.ds(i * cw, cw)], gath.at[z, i], loc_sem.at[i])
        for i in range(CHUNKS)
    ]
    for cp in g_copies:
        cp.start()
    for cp in w_copies:
        cp.start()

    down_pad[...] = jnp.zeros_like(down_pad)
    down_pad[:rank, :] = down_ref[...]
    mix_send[...] = dot(ao_ref[...], down_pad[...], NT).reshape(mix_send.shape)

    barrier = pltpu.get_barrier_semaphore()
    for k in range(1, ctx_n):
        pl.semaphore_signal(
            barrier, inc=1, device_id={"ctx": lax.rem(c + k, ctx_n), "tp": z}, device_id_type=MESH
        )
    for k in range(1, tp_n):
        pl.semaphore_signal(
            barrier, inc=1, device_id={"ctx": c, "tp": lax.rem(z + k, tp_n)}, device_id_type=MESH
        )
    pl.semaphore_wait(barrier, ctx_n - 1 + tp_n - 1)

    def ctx_copy(k, src, dst, s, r):
        return pltpu.make_async_remote_copy(
            src_ref=src, dst_ref=dst, send_sem=s.at[k], recv_sem=r.at[k],
            device_id={"ctx": lax.rem(c + k, ctx_n), "tp": z}, device_id_type=MESH,
        )

    def tp_copy(k, src, dst, s, r):
        return pltpu.make_async_remote_copy(
            src_ref=src, dst_ref=dst, send_sem=s.at[k], recv_sem=r.at[k],
            device_id={"ctx": c, "tp": lax.rem(z + k, tp_n)}, device_id_type=MESH,
        )

    def right_copy(s, i):
        return pltpu.make_async_remote_copy(
            src_ref=gath.at[z - s, i], dst_ref=gath.at[z - s, i],
            send_sem=gr_s.at[s, i], recv_sem=gr_r.at[s, i],
            device_id={"ctx": c, "tp": z + 1}, device_id_type=MESH,
        )

    def left_copy(s, i):
        return pltpu.make_async_remote_copy(
            src_ref=gath.at[z + s, i], dst_ref=gath.at[z + s, i],
            send_sem=gl_s.at[s, i], recv_sem=gl_r.at[s, i],
            device_id={"ctx": c, "tp": z - 1}, device_id_type=MESH,
        )

    def sends_right(s, i):
        last = tp_n - 1 if i >= kept else tp_n
        return jnp.logical_and(z - s >= 0, z + 1 < last)

    def sends_left(s, i):
        first = 1 if i >= kept else 0
        return jnp.logical_and(z + s < tp_n, z - 1 >= first)

    mix_copies = [
        tp_copy(k, mix_send.at[lax.rem(z + k, tp_n)], mix_recv.at[z], mix_s, mix_r)
        for k in range(1, tp_n)
    ]
    for cp in mix_copies:
        cp.start()
    mix_recv[z] = mix_send[z]

    moved = moved_chunks(tp_n)
    kept = CHUNKS - moved
    proj = w_hbm.shape[0]
    wr = proj // ctx_n
    is_edge = jnp.logical_or(z == 0, z == tp_n - 1)
    is_helper = jnp.logical_or(z == 1, z == tp_n - 2)
    inward = jnp.where(z == 0, 1, -1)
    beyond = jnp.where(z == 1, 1, -1)

    def wx_rows(j):
        return wx.at[:, pl.ds(pl.multiple_of(j * wr, wr), wr), :]

    edge_copy = None
    if moved:
        edge_copy = pltpu.make_async_remote_copy(
            src_ref=w.at[pl.ds(kept, moved), pl.ds(pl.multiple_of(c * wr, wr), wr), :],
            dst_ref=wx_rows(c), send_sem=we_s, recv_sem=we_r,
            device_id={"ctx": c, "tp": z + inward}, device_id_type=MESH,
        )

    def out_right(t, more=True):
        s, i = divmod(t, CHUNKS)
        if s < tp_n - 1:
            @pl.when(jnp.logical_and(sends_right(s, i), more))
            def _():
                right_copy(s, i).start()

    def out_left(t, more=True):
        s, i = divmod(t, CHUNKS)
        if s < tp_n - 1:
            @pl.when(jnp.logical_and(sends_left(s, i), more))
            def _():
                left_copy(s, i).start()

    for i in range(CHUNKS):
        g_copies[i].wait()
        if i < AHEAD:
            out_right(i)
            out_left(i)

    for cp in w_copies:
        cp.wait()
    sibling = c + 1 - 2 * lax.rem(c, 2)
    chips = ctx_n // 2

    def sibling_copy(src, dst, s, r):
        return pltpu.make_async_remote_copy(
            src_ref=src, dst_ref=dst, send_sem=s, recv_sem=r,
            device_id={"ctx": sibling, "tp": z}, device_id_type=MESH,
        )

    def shared_gather(at, s, r):
        out = [ctx_copy(2 * k, at(c), at(c), s, r) for k in range(1, chips)]
        on = []
        for k in range(chips):
            block = at(lax.rem(c + ctx_n - 2 * k, ctx_n))
            on.append(sibling_copy(block, block, s.at[2 * k + 1], r.at[2 * k + 1]))
        return out, on

    def hand_over(out, on):
        for k in range(1, chips):
            out[k - 1].wait_recv()
            on[k].start()

    kv[c, 0] = k_ref[...]
    kv[c, 1] = v_ref[...]
    kv_out, kv_on = shared_gather(lambda j: kv.at[j], kv_s, kv_r)
    for cp in kv_out + kv_on[:1]:
        cp.start()

    cot_own = jnp.zeros((blk, rank), F32)
    for i in range(CHUNKS):
        cot_own += dot(gath[z, i], up_ref[:, i * cw : (i + 1) * cw], NT)
    cot[z] = jnp.zeros((blk, cot.shape[2]), BF16)
    cot[z, :, :rank] = cot_own.astype(BF16)
    cot_copies = [tp_copy(k, cot.at[z], cot.at[z], cot_s, cot_r) for k in range(1, tp_n)]
    for cp in cot_copies:
        cp.start()

    for part in range(2):
        for h in range(heads):
            q_st[part, h * half : (h + 1) * half, :] = q_ref[
                part * half : (part + 1) * half, h * hd : (h + 1) * hd
            ]
            ln_st[part, :, h * half : (h + 1) * half] = ln_ref[
                h : h + 1, part * half : (part + 1) * half
            ]
    dq_st[...] = jnp.zeros_like(dq_st)
    dkv_acc[...] = jnp.zeros_like(dkv_acc)

    def project(b, i):
        dacc[b] += dot(gath[b, i], w[i], NT)

    dacc[...] = jnp.zeros_like(dacc)

    def place(pair):
        early = pair <= c
        cell = jnp.where(early, pair, pair - c - 1)
        part = jnp.where(early, 0, 1)
        late_cell = cell >= ctx_n
        dev = jnp.where(late_cell, cells - 1 - cell, cell)
        start = pl.multiple_of(jnp.where(late_cell, half, 0), half)
        return early, cell, part, dev, start

    ctx_up_copies = [
        ctx_copy(k, u_send.at[lax.rem(c + k, ctx_n)], u_recv.at[c], u_s, u_r)
        for k in range(1, ctx_n)
    ]
    d_copies = [ctx_copy(k, d_recv.at[c], d_recv.at[c], d_s, d_r) for k in range(1, ctx_n)]
    rq = uz.shape[1]
    scattered = rq < rank

    def u_rows(t):
        return u_sum.at[pl.ds(pl.multiple_of(t * rq, rq), rq), :] if scattered else u_sum

    uz_copies = [
        tp_copy(k, u_rows(lax.rem(z + k, tp_n)), uz.at[z], uz_s, uz_r) for k in range(1, tp_n)
    ]
    uc_copies = []
    if scattered:
        uc_copies = [tp_copy(k, uc.at[z], uc.at[z], uc_s, uc_r) for k in range(1, tp_n)]
    ua_out, ua_on = shared_gather(lambda j: u_all.at[j], ua_s, ua_r)

    def first_parts():
        for cp in mix_copies:
            cp.wait_recv()
        mixed = mix_recv[0]
        for t in range(1, tp_n):
            mixed += mix_recv[t]
        mixed = mixed.astype(BF16)
        for j in range(ctx_n):
            i, off = (j * uw) // cw, (j * uw) % cw
            part = dot(mixed, gath[z, i, :, off : off + uw], TN)
            u_send[j] = (adapter_scale_factor * part[:rank]).astype(BF16)
        for cp in ctx_up_copies:
            cp.start()
        u_recv[c] = u_send[c]

    def down_parts():
        for cp in cot_copies:
            cp.wait_recv()
        cot_rows = cot[...].reshape(rows, cot.shape[2])
        part = dot(cot_rows, ao_ref[...], TN)
        d_recv[c] = (adapter_scale_factor * part[:rank]).astype(BF16)
        for cp in d_copies:
            cp.start()

    def probabilities():
        for cp in kv_on:
            cp.wait_recv()

        def body(pair, _):
            early, cell, part, dev, start = place(pair)
            keys = kv[dev, 0, pl.ds(start, half), :]
            scores = dot(keys, q_st[part], NT) * scale
            q_cell = jnp.where(early, c, cells - 1 - c)
            shape = (half, half)
            key_pos = cell * half + lax.broadcasted_iota(jnp.int32, shape, 0)
            q_pos = q_cell * half + lax.broadcasted_iota(jnp.int32, shape, 1)
            seen = q_pos >= key_pos
            for h in range(heads):
                cols = slice(h * half, (h + 1) * half)
                p = jnp.exp(scores[:, cols] - ln_st[part, :, cols])
                probs[pair, :, cols] = jnp.where(seen, p, 0.0)
            return 0

        lax.fori_loop(0, cells + 1, body, 0)

    def second_parts():
        for cp in ctx_up_copies:
            cp.wait_recv()
        total = u_recv[0].astype(F32)
        for j in range(1, ctx_n):
            total += u_recv[j].astype(F32)
        u_sum[...] = total.astype(BF16)
        for cp in uz_copies:
            cp.start()
        uz[z] = u_rows(z)[...]
        for cp in d_copies:
            cp.wait_recv()
        total = d_recv[0].astype(F32)
        for j in range(1, ctx_n):
            total += d_recv[j].astype(F32)
        down_out[...] = total

    def third_parts():
        for cp in uz_copies:
            cp.wait_recv()
        total = uz[0].astype(F32)
        for t in range(1, tp_n):
            total += uz[t].astype(F32)
        if scattered:
            uc[z] = total.astype(BF16)
            for cp in uc_copies:
                cp.start()
        else:
            u_all[c] = total.astype(BF16)

    def fourth_parts():
        if scattered:
            for cp in uc_copies:
                cp.wait_recv()
            u_all[c] = uc[...].reshape(u_all.shape[1:])
        for cp in ua_out + ua_on[:1]:
            cp.start()

    wa_copies, wf_copies = [], []
    if moved:
        wa_copies, wf_copies = shared_gather(wx_rows, wa_s, wa_r)

    others = pl.ds(0, tp_n - 1)
    px_base = jnp.where(z < tp_n // 2, 1, 0)
    px_copy = None
    if moved:
        px_copy = pltpu.make_async_remote_copy(
            src_ref=px_send.at[others], dst_ref=px_recv.at[others], send_sem=px_s.at[0],
            recv_sem=px_r.at[0], device_id={"ctx": c, "tp": z - beyond}, device_id_type=MESH,
        )

    def weight_in():
        if moved:
            @pl.when(is_helper)
            def _():
                edge_copy.wait_recv()
                for cp in wa_copies:
                    cp.start()
                wf_copies[0].start()

    def weight_on():
        if moved:
            @pl.when(is_helper)
            def _():
                hand_over(wa_copies, wf_copies)

    def weight_whole():
        if moved:
            @pl.when(is_helper)
            def _():
                for cp in wf_copies:
                    cp.wait_recv()

    def help_out():
        if moved:
            @pl.when(is_helper)
            def _():
                part = jnp.zeros(((tp_n - 1) * blk, proj), F32)
                for i in range(moved):
                    g_rows = gath[pl.ds(px_base, tp_n - 1), kept + i]
                    part += dot(g_rows.reshape((tp_n - 1) * blk, cw), wx[i], NT)
                px_send[: tp_n - 1] = part.astype(BF16).reshape(tp_n - 1, blk, proj)
                px_copy.start()

    edge_right = jnp.logical_and(z + 1 == tp_n - 1, moved > 0)
    edge_left = jnp.logical_and(z - 1 == 0, moved > 0)
    for s in range(tp_n - 1):
        for i in range(CHUNKS):
            got_left = jnp.logical_and(z - 1 - s >= 0, z < (tp_n - 1 if i >= kept else tp_n))
            got_right = jnp.logical_and(z + 1 + s < tp_n, z > (0 if i >= kept else -1))

            @pl.when(got_left)
            def _(s=s, i=i):
                right_copy(s, i).wait_recv()

            @pl.when(got_right)
            def _(s=s, i=i):
                left_copy(s, i).wait_recv()

            t = s * CHUNKS + i
            first = t + AHEAD < CHUNKS
            out_right(t + AHEAD, first or jnp.logical_not(edge_right))
            out_left(t + AHEAD, first or jnp.logical_not(edge_left))
            out_right(t + CHUNKS, edge_right)
            out_left(t + CHUNKS, edge_left)
            if moved and t == CHUNKS - AHEAD:
                @pl.when(is_edge)
                def _():
                    edge_copy.start()
            if s == 0:
                project(z, i)

            @pl.when(got_left)
            def _(s=s, i=i):
                project(z - 1 - s, i)

            @pl.when(got_right)
            def _(s=s, i=i):
                project(z + 1 + s, i)

            if s == 0 and i == 1:
                first_parts()
            if s == 0 and i == 4:
                down_parts()
            if s == 0 and i == 6:
                hand_over(kv_out, kv_on)
            if s == 1 and i == 0:
                probabilities()
            if s == 1 and i == 2:
                weight_in()
            if s == 1 and i == 4:
                second_parts()
            if s == 1 and i == 6:
                third_parts()
            if s == 1 and i == CHUNKS - 1:
                weight_on()
                weight_whole()
                help_out()
            if s == 2 and i == 2:
                fourth_parts()

    if moved:
        @pl.when(is_edge)
        def _():
            px_copy.wait_recv()
            dacc[pl.ds(px_base, tp_n - 1)] += px_recv[: tp_n - 1].astype(F32)

    cot_rows = cot[...].reshape(rows, cot.shape[2])
    d_attn = dacc[...].reshape(rows, dacc.shape[2]) + adapter_scale_factor * dot(
        cot_rows, down_pad[...]
    )
    d_attn = d_attn.astype(BF16)
    for part in range(2):
        for h in range(heads):
            r0, c0 = part * half, h * hd
            block = d_attn[r0 : r0 + half, c0 : c0 + hd]
            do_st[part, h * half : (h + 1) * half, :] = block
            prod = block.astype(F32) * ao_ref[r0 : r0 + half, c0 : c0 + hd].astype(F32)
            delta_st[part, :, h * half : (h + 1) * half] = jnp.sum(prod.T, axis=0, keepdims=True)

    def backward(pair, _):
        early, cell, part, dev, start = place(pair)
        keys = kv[dev, 0, pl.ds(start, half), :]
        values = kv[dev, 1, pl.ds(start, half), :]
        p = probs[pair]
        grads = do_st[part]
        prob_grad = dot(values, grads, NT)
        score_grad = (p * (prob_grad - delta_st[part])).astype(BF16)
        dkv_acc[dev, 1, pl.ds(start, half), :] += dot(p.astype(BF16), grads)
        dkv_acc[dev, 0, pl.ds(start, half), :] += dot(score_grad, q_st[part])
        dq_st[part] += dot(score_grad, keys, TN)
        return 0

    lax.fori_loop(0, cells + 1, backward, 0, unroll=True)

    side = lax.rem(c, 2)
    chip = c // 2
    half_copy = sibling_copy(dkv_send.at[1 - side], dkv_recv.at[0], half_s, half_r)
    for m in range(chips):
        dkv_send[1 - side, m, 0] = (dkv_acc[2 * m + 1 - side, 0] * scale).astype(BF16)
        dkv_send[1 - side, m, 1] = dkv_acc[2 * m + 1 - side, 1].astype(BF16)
    half_copy.start()
    hand_over(ua_out, ua_on)
    half_copy.wait_recv()
    dkv_copies = []
    for k in list(range(1, chips)) + [0]:
        m = lax.rem(chip + k, chips)
        for n, factor in ((0, scale), (1, 1.0)):
            sums = dkv_acc[2 * m + side, n] * factor + dkv_recv[0, m, n].astype(F32)
            if k:
                dkv_send[side, m, n] = sums.astype(BF16)
            else:
                dkv_recv[1, m, n] = sums.astype(BF16)
        if k:
            dkv_copies.append(
                ctx_copy(2 * k, dkv_send.at[side, m], dkv_recv.at[1, chip], dkv_s, dkv_r)
            )
            dkv_copies[-1].start()

    for part in range(2):
        for h in range(heads):
            dq_out[part * half : (part + 1) * half, h * hd : (h + 1) * hd] = (
                dq_st[part, h * half : (h + 1) * half, :] * scale
            ).astype(BF16)
    for cp in ua_on:
        cp.wait_recv()
    for j in range(ctx_n):
        up_out[:, j * uw : (j + 1) * uw] = u_all[j]

    for cp in dkv_copies:
        cp.wait_recv()
    total = dkv_recv[1, 0].astype(F32)
    for m in range(1, chips):
        total += dkv_recv[1, m].astype(F32)
    pair_buf[0] = total.astype(BF16)
    other = z + 1 - 2 * lax.rem(z, 2)
    pair_copy = pltpu.make_async_remote_copy(
        src_ref=pair_buf.at[0], dst_ref=pair_buf.at[1], send_sem=pair_s, recv_sem=pair_r,
        device_id={"ctx": c, "tp": other}, device_id_type=MESH,
    )
    pair_copy.start()
    pair_copy.wait_recv()
    sums = pair_buf[0].astype(F32) + pair_buf[1].astype(F32)
    dk_out[...] = sums[0].astype(BF16)
    dv_out[...] = sums[1].astype(BF16)

    for group in (
        kv_out, kv_on, cot_copies, mix_copies, ctx_up_copies, d_copies, uz_copies, uc_copies,
        ua_out, ua_on, [half_copy], dkv_copies,
    ):
        for cp in group:
            cp.wait_send()
    pair_copy.wait_send()
    if moved:
        @pl.when(is_edge)
        def _():
            edge_copy.wait_send()

        @pl.when(is_helper)
        def _():
            for cp in wa_copies + wf_copies:
                cp.wait_send()
            px_copy.wait_send()
    for s in range(tp_n - 1):
        for i in range(CHUNKS):
            @pl.when(sends_right(s, i))
            def _(s=s, i=i):
                right_copy(s, i).wait_send()

            @pl.when(sends_left(s, i))
            def _(s=s, i=i):
                left_copy(s, i).wait_send()


def moved_chunks(tp_n):
    return MOVED if tp_n == 4 else 0


def hand_on(*refs):
    n = len(refs) // 2
    for i in range(n):
        refs[n + i][...] = refs[i][...]


def handed_on(*arrays):
    vmem = pl.BlockSpec(memory_space=pltpu.VMEM)
    return pl.pallas_call(
        hand_on,
        out_shape=tuple(jax.ShapeDtypeStruct(a.shape, a.dtype) for a in arrays),
        in_specs=[vmem] * len(arrays),
        out_specs=(vmem,) * len(arrays),
    )(*arrays)


def local(q, k, v, ao, ln, g, w, down, up):
    ctx_n = lax.axis_size("ctx")
    tp_n = lax.axis_size("tp")
    rows, q_cols = q.shape
    heads = ln.shape[0]
    hd = q_cols // heads
    half = rows // 2
    blk = rows // tp_n
    width = g.shape[1]
    cw = width // CHUNKS
    uw = width // ctx_n
    proj = w.shape[0]
    rank = down.shape[1]
    moves = moved_chunks(tp_n) > 0
    rq = rank // tp_n if rank % (16 * tp_n) == 0 else rank
    lanes = max(128, rank)
    pairs = 2 * ctx_n + 1
    vmem = pl.BlockSpec(memory_space=pltpu.VMEM)
    hbm = pl.BlockSpec(memory_space=pl.ANY)
    V = pltpu.VMEM
    DMA = pltpu.SemaphoreType.DMA
    scratch = [
        V((tp_n, CHUNKS, blk, cw), BF16),
        V((CHUNKS, proj, cw), BF16),
        V((tp_n, blk, proj), F32),
        V((lanes, proj), BF16),
        V((tp_n, blk, lanes), BF16),
        V((tp_n, blk, lanes), F32),
        V((tp_n, blk, lanes), F32),
        V((ctx_n, rank, uw), BF16),
        V((ctx_n, rank, uw), BF16),
        V((rank, uw), BF16),
        V((tp_n, rq, uw), BF16),
        V((tp_n, rq, uw), BF16),
        V((ctx_n, rank, uw), BF16),
        V((MOVED, proj, cw) if moves else (1, 16, 128), BF16),
        V((tp_n, blk, proj) if moves else (1, 16, 128), BF16),
        V((tp_n, blk, proj) if moves else (1, 16, 128), BF16),
        V((ctx_n, rank, proj), BF16),
        V((ctx_n, 2, rows, hd), BF16),
        V((pairs, half, heads * half), F32),
        V((2, heads * half, hd), BF16),
        V((2, heads * half, hd), BF16),
        V((2, 1, heads * half), F32),
        V((2, 1, heads * half), F32),
        V((2, heads * half, hd), F32),
        V((ctx_n, 2, rows, hd), F32),
        V((2, ctx_n // 2, 2, rows, hd), BF16),
        V((2, ctx_n // 2, 2, rows, hd), BF16),
        V((2, 2, rows, hd), BF16),
        DMA((2 * CHUNKS,)),
    ]
    scratch += [DMA((tp_n, CHUNKS))] * 4
    scratch += [DMA((ctx_n,))] * 2 + [DMA((tp_n,))] * 4 + [DMA((ctx_n,))] * 2
    scratch += [DMA((tp_n,))] * 4 + [DMA((ctx_n,))] * 6 + [DMA((tp_n,))] * 2
    scratch += [DMA((ctx_n,))] * 2 + [DMA] * 6
    dq, dk, dv, dd, du = pl.pallas_call(
        functools.partial(kernel, ctx_n, tp_n, heads),
        out_shape=(
            jax.ShapeDtypeStruct(q.shape, BF16),
            jax.ShapeDtypeStruct(k.shape, BF16),
            jax.ShapeDtypeStruct(v.shape, BF16),
            jax.ShapeDtypeStruct((rank, proj), F32),
            jax.ShapeDtypeStruct(up.shape, BF16),
        ),
        in_specs=[vmem] * 5 + [hbm] * 2 + [vmem] * 2,
        out_specs=(vmem,) * 5,
        scratch_shapes=scratch,
        compiler_params=pltpu.CompilerParams(
            collective_id=0, has_side_effects=True, vmem_limit_bytes=60 * 2**20
        ),
        cost_estimate=pl.CostEstimate(
            flops=5 * 10**9, bytes_accessed=16 * 2**20, transcendentals=2**21
        ),
    )(q, k, v, ao, ln, g, w, down.T, up)
    dq, dk, dv, dd, du = handed_on(dq, dk, dv, dd, du)
    return dq, dk, dv, dd.T, du


def solution(mesh):
    placed = (
        P("ctx", "tp"),
        P("ctx", "tp"),
        P("ctx", "tp"),
        P("ctx", "tp"),
        P("tp", "ctx"),
        P(("ctx", "tp"), None),
        P("tp", None),
        P("tp", None),
        P(),
    )
    return jax.shard_map(
        local,
        mesh=mesh,
        in_specs=placed,
        out_specs=(P("ctx", "tp"), P("ctx", "tp"), P("ctx", "tp"), P("tp", None), P()),
        check_vma=False,
    )
```

```python
import functools

import jax
import jax.numpy as jnp
from jax import lax
from jax.experimental import pallas as pl
from jax.experimental.pallas import tpu as pltpu
from jax.sharding import PartitionSpec as P

adapter_scale_factor = 2.0
MESH = pl.DeviceIdType.MESH
F32 = jnp.float32
BF16 = jnp.bfloat16
NT = (((1,), (1,)), ((), ()))
TN = (((0,), (0,)), ((), ()))
CHUNKS = 8
AHEAD = 3
MOVED = 2
KEPT = CHUNKS - MOVED


def dot(a, b, dims=(((1,), (0,)), ((), ()))):
    return lax.dot_general(a, b, dims, preferred_element_type=F32)


def kernel(
    ctx_n, tp_n, heads,
    q_ref, k_ref, v_ref, ao_ref, ln_ref, g_hbm, w_hbm, down_ref, up_ref,
    dq_out, dk_out, dv_out, down_out, up_out,
    gath, w, dacc, down_pad,
    cot, mix_send, mix_recv,
    u_send, u_recv, u_sum, uz, uc, u_all, wx, px_send, px_recv,
    d_recv, kv, probs, q_st, do_st, ln_st, delta_st, dq_st,
    dkv_acc, dkv_send, dkv_recv, pair_buf,
    loc_sem, gr_s, gr_r, gl_s, gl_r,
    kv_s, kv_r, cot_s, cot_r, mix_s, mix_r, u_s, u_r, uz_s, uz_r, uc_s, uc_r, ua_s, ua_r,
    d_s, d_r, dkv_s, dkv_r, px_s, px_r, wa_s, wa_r, half_s, half_r, we_s, we_r, pair_s, pair_r,
):
    c = lax.axis_index("ctx")
    z = lax.axis_index("tp")
    rows = q_ref.shape[0]
    half = rows // 2
    blk = rows // tp_n
    width = g_hbm.shape[1]
    cw = width // CHUNKS
    uw = width // ctx_n
    rank = down_ref.shape[0]
    hd = q_ref.shape[1] // heads
    scale = hd ** (-0.5)
    cells = 2 * ctx_n

    w_copies = [
        pltpu.make_async_copy(
            w_hbm.at[:, pl.ds(i * cw, cw)], w.at[i], loc_sem.at[CHUNKS + i]
        )
        for i in range(CHUNKS)
    ]
    g_copies = [
        pltpu.make_async_copy(g_hbm.at[:, pl.ds(i * cw, cw)], gath.at[z, i], loc_sem.at[i])
        for i in range(CHUNKS)
    ]
    for cp in g_copies:
        cp.start()
    for cp in w_copies:
        cp.start()

    down_pad[...] = jnp.zeros_like(down_pad)
    down_pad[:rank, :] = down_ref[...]
    mix_send[...] = dot(ao_ref[...], down_pad[...], NT).reshape(mix_send.shape)

    barrier = pltpu.get_barrier_semaphore()
    for k in range(1, ctx_n):
        pl.semaphore_signal(
            barrier, inc=1, device_id={"ctx": lax.rem(c + k, ctx_n), "tp": z}, device_id_type=MESH
        )
    for k in range(1, tp_n):
        pl.semaphore_signal(
            barrier, inc=1, device_id={"ctx": c, "tp": lax.rem(z + k, tp_n)}, device_id_type=MESH
        )
    pl.semaphore_wait(barrier, ctx_n - 1 + tp_n - 1)

    def ctx_copy(k, src, dst, s, r):
        return pltpu.make_async_remote_copy(
            src_ref=src, dst_ref=dst, send_sem=s.at[k], recv_sem=r.at[k],
            device_id={"ctx": lax.rem(c + k, ctx_n), "tp": z}, device_id_type=MESH,
        )

    def tp_copy(k, src, dst, s, r):
        return pltpu.make_async_remote_copy(
            src_ref=src, dst_ref=dst, send_sem=s.at[k], recv_sem=r.at[k],
            device_id={"ctx": c, "tp": lax.rem(z + k, tp_n)}, device_id_type=MESH,
        )

    def right_copy(s, i):
        return pltpu.make_async_remote_copy(
            src_ref=gath.at[z - s, i], dst_ref=gath.at[z - s, i],
            send_sem=gr_s.at[s, i], recv_sem=gr_r.at[s, i],
            device_id={"ctx": c, "tp": z + 1}, device_id_type=MESH,
        )

    def left_copy(s, i):
        return pltpu.make_async_remote_copy(
            src_ref=gath.at[z + s, i], dst_ref=gath.at[z + s, i],
            send_sem=gl_s.at[s, i], recv_sem=gl_r.at[s, i],
            device_id={"ctx": c, "tp": z - 1}, device_id_type=MESH,
        )

    def sends_right(s, i):
        last = tp_n - 1 if i >= kept else tp_n
        return jnp.logical_and(z - s >= 0, z + 1 < last)

    def sends_left(s, i):
        first = 1 if i >= kept else 0
        return jnp.logical_and(z + s < tp_n, z - 1 >= first)

    mix_copies = [
        tp_copy(k, mix_send.at[lax.rem(z + k, tp_n)], mix_recv.at[z], mix_s, mix_r)
        for k in range(1, tp_n)
    ]
    for cp in mix_copies:
        cp.start()
    mix_recv[z] = mix_send[z]

    moved = moved_chunks(tp_n)
    kept = CHUNKS - moved
    proj = w_hbm.shape[0]
    wr = proj // ctx_n
    is_edge = jnp.logical_or(z == 0, z == tp_n - 1)
    is_helper = jnp.logical_or(z == 1, z == tp_n - 2)
    inward = jnp.where(z == 0, 1, -1)
    beyond = jnp.where(z == 1, 1, -1)

    def wx_rows(j):
        return wx.at[:, pl.ds(pl.multiple_of(j * wr, wr), wr), :]

    edge_copy = None
    if moved:
        edge_copy = pltpu.make_async_remote_copy(
            src_ref=w.at[pl.ds(kept, moved), pl.ds(pl.multiple_of(c * wr, wr), wr), :],
            dst_ref=wx_rows(c), send_sem=we_s, recv_sem=we_r,
            device_id={"ctx": c, "tp": z + inward}, device_id_type=MESH,
        )

    def out_right(t, more=True):
        s, i = divmod(t, CHUNKS)
        if s < tp_n - 1:
            @pl.when(jnp.logical_and(sends_right(s, i), more))
            def _():
                right_copy(s, i).start()

    def out_left(t, more=True):
        s, i = divmod(t, CHUNKS)
        if s < tp_n - 1:
            @pl.when(jnp.logical_and(sends_left(s, i), more))
            def _():
                left_copy(s, i).start()

    for i in range(CHUNKS):
        g_copies[i].wait()
        if i < AHEAD:
            out_right(i)
            out_left(i)

    for cp in w_copies:
        cp.wait()
    sibling = c + 1 - 2 * lax.rem(c, 2)
    chips = ctx_n // 2

    def sibling_copy(src, dst, s, r):
        return pltpu.make_async_remote_copy(
            src_ref=src, dst_ref=dst, send_sem=s, recv_sem=r,
            device_id={"ctx": sibling, "tp": z}, device_id_type=MESH,
        )

    def shared_gather(at, s, r):
        out = [ctx_copy(2 * k, at(c), at(c), s, r) for k in range(1, chips)]
        on = []
        for k in range(chips):
            block = at(lax.rem(c + ctx_n - 2 * k, ctx_n))
            on.append(sibling_copy(block, block, s.at[2 * k + 1], r.at[2 * k + 1]))
        return out, on

    def hand_over(out, on):
        for k in range(1, chips):
            out[k - 1].wait_recv()
            on[k].start()

    kv[c, 0] = k_ref[...]
    kv[c, 1] = v_ref[...]
    kv_out, kv_on = shared_gather(lambda j: kv.at[j], kv_s, kv_r)
    for cp in kv_out + kv_on[:1]:
        cp.start()

    cot_own = jnp.zeros((blk, rank), F32)
    for i in range(CHUNKS):
        cot_own += dot(gath[z, i], up_ref[:, i * cw : (i + 1) * cw], NT)
    cot[z] = jnp.zeros((blk, cot.shape[2]), BF16)
    cot[z, :, :rank] = cot_own.astype(BF16)
    cot_copies = [tp_copy(k, cot.at[z], cot.at[z], cot_s, cot_r) for k in range(1, tp_n)]
    for cp in cot_copies:
        cp.start()

    for part in range(2):
        for h in range(heads):
            q_st[part, h * half : (h + 1) * half, :] = q_ref[
                part * half : (part + 1) * half, h * hd : (h + 1) * hd
            ]
            ln_st[part, :, h * half : (h + 1) * half] = ln_ref[
                h : h + 1, part * half : (part + 1) * half
            ]
    dq_st[...] = jnp.zeros_like(dq_st)
    dkv_acc[...] = jnp.zeros_like(dkv_acc)

    def project(b, i):
        dacc[b] += dot(gath[b, i], w[i], NT)

    dacc[...] = jnp.zeros_like(dacc)

    def place(pair):
        early = pair <= c
        cell = jnp.where(early, pair, pair - c - 1)
        part = jnp.where(early, 0, 1)
        late_cell = cell >= ctx_n
        dev = jnp.where(late_cell, cells - 1 - cell, cell)
        start = pl.multiple_of(jnp.where(late_cell, half, 0), half)
        return early, cell, part, dev, start

    ctx_up_copies = [
        ctx_copy(k, u_send.at[lax.rem(c + k, ctx_n)], u_recv.at[c], u_s, u_r)
        for k in range(1, ctx_n)
    ]
    d_copies = [ctx_copy(k, d_recv.at[c], d_recv.at[c], d_s, d_r) for k in range(1, ctx_n)]
    rq = uz.shape[1]
    scattered = rq < rank

    def u_rows(t):
        return u_sum.at[pl.ds(pl.multiple_of(t * rq, rq), rq), :] if scattered else u_sum

    uz_copies = [
        tp_copy(k, u_rows(lax.rem(z + k, tp_n)), uz.at[z], uz_s, uz_r) for k in range(1, tp_n)
    ]
    uc_copies = []
    if scattered:
        uc_copies = [tp_copy(k, uc.at[z], uc.at[z], uc_s, uc_r) for k in range(1, tp_n)]
    ua_out, ua_on = shared_gather(lambda j: u_all.at[j], ua_s, ua_r)

    def first_parts():
        for cp in mix_copies:
            cp.wait_recv()
        mixed = mix_recv[0]
        for t in range(1, tp_n):
            mixed += mix_recv[t]
        mixed = mixed.astype(BF16)
        for j in range(ctx_n):
            i, off = (j * uw) // cw, (j * uw) % cw
            part = dot(mixed, gath[z, i, :, off : off + uw], TN)
            u_send[j] = (adapter_scale_factor * part[:rank]).astype(BF16)
        for cp in ctx_up_copies:
            cp.start()
        u_recv[c] = u_send[c]

    def down_parts():
        for cp in cot_copies:
            cp.wait_recv()
        cot_rows = cot[...].reshape(rows, cot.shape[2])
        part = dot(cot_rows, ao_ref[...], TN)
        d_recv[c] = (adapter_scale_factor * part[:rank]).astype(BF16)
        for cp in d_copies:
            cp.start()

    def probabilities():
        for cp in kv_on:
            cp.wait_recv()

        def body(pair, _):
            early, cell, part, dev, start = place(pair)
            keys = kv[dev, 0, pl.ds(start, half), :]
            scores = dot(keys, q_st[part], NT) * scale
            q_cell = jnp.where(early, c, cells - 1 - c)
            shape = (half, half)
            key_pos = cell * half + lax.broadcasted_iota(jnp.int32, shape, 0)
            q_pos = q_cell * half + lax.broadcasted_iota(jnp.int32, shape, 1)
            seen = q_pos >= key_pos
            for h in range(heads):
                cols = slice(h * half, (h + 1) * half)
                p = jnp.exp(scores[:, cols] - ln_st[part, :, cols])
                probs[pair, :, cols] = jnp.where(seen, p, 0.0)
            return 0

        lax.fori_loop(0, cells + 1, body, 0)

    def second_parts():
        for cp in ctx_up_copies:
            cp.wait_recv()
        total = u_recv[0].astype(F32)
        for j in range(1, ctx_n):
            total += u_recv[j].astype(F32)
        u_sum[...] = total.astype(BF16)
        for cp in uz_copies:
            cp.start()
        uz[z] = u_rows(z)[...]
        for cp in d_copies:
            cp.wait_recv()
        total = d_recv[0].astype(F32)
        for j in range(1, ctx_n):
            total += d_recv[j].astype(F32)
        down_out[...] = total

    def third_parts():
        for cp in uz_copies:
            cp.wait_recv()
        total = uz[0].astype(F32)
        for t in range(1, tp_n):
            total += uz[t].astype(F32)
        if scattered:
            uc[z] = total.astype(BF16)
            for cp in uc_copies:
                cp.start()
        else:
            u_all[c] = total.astype(BF16)

    def fourth_parts():
        if scattered:
            for cp in uc_copies:
                cp.wait_recv()
            u_all[c] = uc[...].reshape(u_all.shape[1:])
        for cp in ua_out + ua_on[:1]:
            cp.start()

    wa_copies, wf_copies = [], []
    if moved:
        wa_copies, wf_copies = shared_gather(wx_rows, wa_s, wa_r)

    others = pl.ds(0, tp_n - 1)
    px_base = jnp.where(z < tp_n // 2, 1, 0)
    px_copy = None
    if moved:
        px_copy = pltpu.make_async_remote_copy(
            src_ref=px_send.at[others], dst_ref=px_recv.at[others], send_sem=px_s.at[0],
            recv_sem=px_r.at[0], device_id={"ctx": c, "tp": z - beyond}, device_id_type=MESH,
        )

    def weight_in():
        if moved:
            @pl.when(is_helper)
            def _():
                edge_copy.wait_recv()
                for cp in wa_copies:
                    cp.start()
                wf_copies[0].start()

    def weight_on():
        if moved:
            @pl.when(is_helper)
            def _():
                hand_over(wa_copies, wf_copies)

    def weight_whole():
        if moved:
            @pl.when(is_helper)
            def _():
                for cp in wf_copies:
                    cp.wait_recv()

    def help_out():
        if moved:
            @pl.when(is_helper)
            def _():
                part = jnp.zeros(((tp_n - 1) * blk, proj), F32)
                for i in range(moved):
                    g_rows = gath[pl.ds(px_base, tp_n - 1), kept + i]
                    part += dot(g_rows.reshape((tp_n - 1) * blk, cw), wx[i], NT)
                px_send[: tp_n - 1] = part.astype(BF16).reshape(tp_n - 1, blk, proj)
                px_copy.start()

    edge_right = jnp.logical_and(z + 1 == tp_n - 1, moved > 0)
    edge_left = jnp.logical_and(z - 1 == 0, moved > 0)
    for s in range(tp_n - 1):
        for i in range(CHUNKS):
            got_left = jnp.logical_and(z - 1 - s >= 0, z < (tp_n - 1 if i >= kept else tp_n))
            got_right = jnp.logical_and(z + 1 + s < tp_n, z > (0 if i >= kept else -1))

            @pl.when(got_left)
            def _(s=s, i=i):
                right_copy(s, i).wait_recv()

            @pl.when(got_right)
            def _(s=s, i=i):
                left_copy(s, i).wait_recv()

            t = s * CHUNKS + i
            first = t + AHEAD < CHUNKS
            out_right(t + AHEAD, first or jnp.logical_not(edge_right))
            out_left(t + AHEAD, first or jnp.logical_not(edge_left))
            out_right(t + CHUNKS, edge_right)
            out_left(t + CHUNKS, edge_left)
            if moved and t == 2:
                @pl.when(is_edge)
                def _():
                    edge_copy.start()
            if s == 0:
                project(z, i)

            @pl.when(got_left)
            def _(s=s, i=i):
                project(z - 1 - s, i)

            @pl.when(got_right)
            def _(s=s, i=i):
                project(z + 1 + s, i)

            if s == 0 and i == 1:
                first_parts()
            if s == 0 and i == 4:
                down_parts()
            if s == 0 and i == 6:
                hand_over(kv_out, kv_on)
            if s == 1 and i == 0:
                probabilities()
            if s == 1 and i == 2:
                weight_in()
            if s == 1 and i == 4:
                second_parts()
            if s == 1 and i == 6:
                third_parts()
            if s == 1 and i == CHUNKS - 1:
                weight_on()
                weight_whole()
                help_out()
            if s == 2 and i == 2:
                fourth_parts()

    if moved:
        @pl.when(is_edge)
        def _():
            px_copy.wait_recv()
            dacc[pl.ds(px_base, tp_n - 1)] += px_recv[: tp_n - 1].astype(F32)

    cot_rows = cot[...].reshape(rows, cot.shape[2])
    d_attn = dacc[...].reshape(rows, dacc.shape[2]) + adapter_scale_factor * dot(
        cot_rows, down_pad[...]
    )
    d_attn = d_attn.astype(BF16)
    for part in range(2):
        for h in range(heads):
            r0, c0 = part * half, h * hd
            block = d_attn[r0 : r0 + half, c0 : c0 + hd]
            do_st[part, h * half : (h + 1) * half, :] = block
            prod = block.astype(F32) * ao_ref[r0 : r0 + half, c0 : c0 + hd].astype(F32)
            delta_st[part, :, h * half : (h + 1) * half] = jnp.sum(prod.T, axis=0, keepdims=True)

    def backward(pair, _):
        early, cell, part, dev, start = place(pair)
        keys = kv[dev, 0, pl.ds(start, half), :]
        values = kv[dev, 1, pl.ds(start, half), :]
        p = probs[pair]
        grads = do_st[part]
        prob_grad = dot(values, grads, NT)
        score_grad = (p * (prob_grad - delta_st[part])).astype(BF16)
        dkv_acc[dev, 1, pl.ds(start, half), :] += dot(p.astype(BF16), grads)
        dkv_acc[dev, 0, pl.ds(start, half), :] += dot(score_grad, q_st[part])
        dq_st[part] += dot(score_grad, keys, TN)
        return 0

    lax.fori_loop(0, cells + 1, backward, 0, unroll=True)

    side = lax.rem(c, 2)
    chip = c // 2
    half_copy = sibling_copy(dkv_send.at[1 - side], dkv_recv.at[0], half_s, half_r)
    for m in range(chips):
        dkv_send[1 - side, m, 0] = (dkv_acc[2 * m + 1 - side, 0] * scale).astype(BF16)
        dkv_send[1 - side, m, 1] = dkv_acc[2 * m + 1 - side, 1].astype(BF16)
    half_copy.start()
    hand_over(ua_out, ua_on)
    half_copy.wait_recv()
    dkv_copies = []
    for k in list(range(1, chips)) + [0]:
        m = lax.rem(chip + k, chips)
        for n, factor in ((0, scale), (1, 1.0)):
            sums = dkv_acc[2 * m + side, n] * factor + dkv_recv[0, m, n].astype(F32)
            if k:
                dkv_send[side, m, n] = sums.astype(BF16)
            else:
                dkv_recv[1, m, n] = sums.astype(BF16)
        if k:
            dkv_copies.append(
                ctx_copy(2 * k, dkv_send.at[side, m], dkv_recv.at[1, chip], dkv_s, dkv_r)
            )
            dkv_copies[-1].start()

    for part in range(2):
        for h in range(heads):
            dq_out[part * half : (part + 1) * half, h * hd : (h + 1) * hd] = (
                dq_st[part, h * half : (h + 1) * half, :] * scale
            ).astype(BF16)
    for cp in ua_on:
        cp.wait_recv()
    for j in range(ctx_n):
        up_out[:, j * uw : (j + 1) * uw] = u_all[j]

    for cp in dkv_copies:
        cp.wait_recv()
    total = dkv_recv[1, 0].astype(F32)
    for m in range(1, chips):
        total += dkv_recv[1, m].astype(F32)
    pair_buf[0] = total.astype(BF16)
    other = z + 1 - 2 * lax.rem(z, 2)
    pair_copy = pltpu.make_async_remote_copy(
        src_ref=pair_buf.at[0], dst_ref=pair_buf.at[1], send_sem=pair_s, recv_sem=pair_r,
        device_id={"ctx": c, "tp": other}, device_id_type=MESH,
    )
    pair_copy.start()
    pair_copy.wait_recv()
    sums = pair_buf[0].astype(F32) + pair_buf[1].astype(F32)
    dk_out[...] = sums[0].astype(BF16)
    dv_out[...] = sums[1].astype(BF16)

    for group in (
        kv_out, kv_on, cot_copies, mix_copies, ctx_up_copies, d_copies, uz_copies, uc_copies,
        ua_out, ua_on, [half_copy], dkv_copies,
    ):
        for cp in group:
            cp.wait_send()
    pair_copy.wait_send()
    if moved:
        @pl.when(is_edge)
        def _():
            edge_copy.wait_send()

        @pl.when(is_helper)
        def _():
            for cp in wa_copies + wf_copies:
                cp.wait_send()
            px_copy.wait_send()
    for s in range(tp_n - 1):
        for i in range(CHUNKS):
            @pl.when(sends_right(s, i))
            def _(s=s, i=i):
                right_copy(s, i).wait_send()

            @pl.when(sends_left(s, i))
            def _(s=s, i=i):
                left_copy(s, i).wait_send()


def moved_chunks(tp_n):
    return MOVED if tp_n == 4 else 0


def hand_on(*refs):
    n = len(refs) // 2
    for i in range(n):
        refs[n + i][...] = refs[i][...]


def handed_on(*arrays):
    vmem = pl.BlockSpec(memory_space=pltpu.VMEM)
    return pl.pallas_call(
        hand_on,
        out_shape=tuple(jax.ShapeDtypeStruct(a.shape, a.dtype) for a in arrays),
        in_specs=[vmem] * len(arrays),
        out_specs=(vmem,) * len(arrays),
    )(*arrays)


def local(q, k, v, ao, ln, g, w, down, up):
    ctx_n = lax.axis_size("ctx")
    tp_n = lax.axis_size("tp")
    rows, q_cols = q.shape
    heads = ln.shape[0]
    hd = q_cols // heads
    half = rows // 2
    blk = rows // tp_n
    width = g.shape[1]
    cw = width // CHUNKS
    uw = width // ctx_n
    proj = w.shape[0]
    rank = down.shape[1]
    moves = moved_chunks(tp_n) > 0
    rq = rank // tp_n if rank % (16 * tp_n) == 0 else rank
    lanes = max(128, rank)
    pairs = 2 * ctx_n + 1
    vmem = pl.BlockSpec(memory_space=pltpu.VMEM)
    hbm = pl.BlockSpec(memory_space=pl.ANY)
    V = pltpu.VMEM
    DMA = pltpu.SemaphoreType.DMA
    scratch = [
        V((tp_n, CHUNKS, blk, cw), BF16),
        V((CHUNKS, proj, cw), BF16),
        V((tp_n, blk, proj), F32),
        V((lanes, proj), BF16),
        V((tp_n, blk, lanes), BF16),
        V((tp_n, blk, lanes), F32),
        V((tp_n, blk, lanes), F32),
        V((ctx_n, rank, uw), BF16),
        V((ctx_n, rank, uw), BF16),
        V((rank, uw), BF16),
        V((tp_n, rq, uw), BF16),
        V((tp_n, rq, uw), BF16),
        V((ctx_n, rank, uw), BF16),
        V((MOVED, proj, cw) if moves else (1, 16, 128), BF16),
        V((tp_n, blk, proj) if moves else (1, 16, 128), BF16),
        V((tp_n, blk, proj) if moves else (1, 16, 128), BF16),
        V((ctx_n, rank, proj), BF16),
        V((ctx_n, 2, rows, hd), BF16),
        V((pairs, half, heads * half), F32),
        V((2, heads * half, hd), BF16),
        V((2, heads * half, hd), BF16),
        V((2, 1, heads * half), F32),
        V((2, 1, heads * half), F32),
        V((2, heads * half, hd), F32),
        V((ctx_n, 2, rows, hd), F32),
        V((2, ctx_n // 2, 2, rows, hd), BF16),
        V((2, ctx_n // 2, 2, rows, hd), BF16),
        V((2, 2, rows, hd), BF16),
        DMA((2 * CHUNKS,)),
    ]
    scratch += [DMA((tp_n, CHUNKS))] * 4
    scratch += [DMA((ctx_n,))] * 2 + [DMA((tp_n,))] * 4 + [DMA((ctx_n,))] * 2
    scratch += [DMA((tp_n,))] * 4 + [DMA((ctx_n,))] * 6 + [DMA((tp_n,))] * 2
    scratch += [DMA((ctx_n,))] * 2 + [DMA] * 6
    dq, dk, dv, dd, du = pl.pallas_call(
        functools.partial(kernel, ctx_n, tp_n, heads),
        out_shape=(
            jax.ShapeDtypeStruct(q.shape, BF16),
            jax.ShapeDtypeStruct(k.shape, BF16),
            jax.ShapeDtypeStruct(v.shape, BF16),
            jax.ShapeDtypeStruct((rank, proj), F32),
            jax.ShapeDtypeStruct(up.shape, BF16),
        ),
        in_specs=[vmem] * 5 + [hbm] * 2 + [vmem] * 2,
        out_specs=(vmem,) * 5,
        scratch_shapes=scratch,
        compiler_params=pltpu.CompilerParams(
            collective_id=0, has_side_effects=True, vmem_limit_bytes=60 * 2**20
        ),
        cost_estimate=pl.CostEstimate(
            flops=5 * 10**9, bytes_accessed=16 * 2**20, transcendentals=2**21
        ),
    )(q, k, v, ao, ln, g, w, down.T, up)
    dq, dk, dv, dd, du = handed_on(dq, dk, dv, dd, du)
    return dq, dk, dv, dd.T, du


def solution(mesh):
    placed = (
        P("ctx", "tp"),
        P("ctx", "tp"),
        P("ctx", "tp"),
        P("ctx", "tp"),
        P("tp", "ctx"),
        P(("ctx", "tp"), None),
        P("tp", None),
        P("tp", None),
        P(),
    )
    return jax.shard_map(
        local,
        mesh=mesh,
        in_specs=placed,
        out_specs=(P("ctx", "tp"), P("ctx", "tp"), P("ctx", "tp"), P("tp", None), P()),
        check_vma=False,
    )
```
